32 devices in a mesh: row: 4 (over x, core), grid: 8 (over z, y).
Axes of the slice: x: 2, y: 2, z: 4, core: 2. Of those that a mesh axis runs over, the one named last changes fastest.
Arguments:
- cholesky: float32 [8, 153600], P('row'), may hold values from -6 to 6
- factor: float32 [1200, 6144], P('row', 'grid'), may hold values from -6 to 6
- core: float32 [6144, 128], P('grid'), may hold values from -0.078125 to 0.078125
Outputs:
- residual: float32 [8, 153600], P('row')
- core_grad: float32 [6144, 128], P('grid')
- factor_grad: float32 [1200, 6144], P('row', 'grid')
The draws below stay inside these ranges and needn't reach their ends.
All inputs are finite; a program needn't handle non-finite values.
Results may differ from the reference program's by a relative error of at most 0.00012.
Values sent between devices are 32-bit elements; how exact they have to be, the bound alone decides.
A program may use at most 64 MiB of HBM per device.

```python
import jax
import jax.numpy as jnp
from jax import lax

N = 1200
G = 6144
K = 128
NP = 8


def block_levels(key, extent, pieces, low, top_value):
    gain, own = 1.0, jax.random.fold_in(key, 6)
    for axis_at, shards_of in pieces:
        steps = jnp.exp(jax.random.uniform(jax.random.fold_in(own, axis_at), (shards_of,), jnp.float32, low / len(pieces), top_value / len(pieces)))
        gain = gain * jnp.repeat(steps, extent[axis_at] // shards_of).reshape([-1 if axis == axis_at else 1 for axis in range(len(extent))])
    return gain


def bell_draw(rng, extent, spread, bound, split=(), held_as=jnp.bfloat16):
    drawn = spread * jax.random.normal(rng, extent, jnp.float32)
    if split:
        drawn = drawn * block_levels(rng, extent, split, -0.22, 0.18)
    return jnp.clip(drawn, -bound, bound).astype(held_as)


def setup_inputs(seed: int = 0) -> dict:
    key_list = jax.random.split(jax.random.key(seed), 4)
    cholesky = bell_draw(key_list[0], (NP, N * K), 1.0, 6.0, ((0, 4),), jnp.float32)
    factor = bell_draw(key_list[1], (N, G), 1.0, 6.0, ((0, 4), (1, 8)), jnp.float32)
    core = bell_draw(key_list[2], (G, K), G ** -0.5, 0.078125, ((0, 8),), jnp.float32)
    return {"cholesky": cholesky, "factor": factor, "core": core}


def reference(cholesky, factor, core):
    hi = lax.Precision.HIGHEST
    count = cholesky.shape[0]
    vectors = core.shape[1]
    slab = cholesky.reshape(count, factor.shape[0], vectors)
    first = factor[:count]
    pair = first[:, None, :] * factor[None, :, :]
    model = jnp.einsum('pqg,gk->pqk', pair, core, precision=hi)
    residual = slab - model
    core_grad = -(1.0 / jnp.sqrt(jnp.float32(count * N))) * jnp.einsum('pqg,pqk->gk', pair, residual, precision=hi)
    proj = jnp.einsum('pqk,gk->pqg', residual, core, precision=hi)
    outer = jnp.einsum('pqg,pg->qg', proj, first, precision=hi)
    inner = jnp.einsum('pqg,qg->pg', proj, factor, precision=hi)
    total = outer.at[:count].add(inner)
    factor_grad = -jnp.sqrt(jnp.float32(G) / jnp.float32(N * K)) * total
    return (residual.reshape(count, -1), core_grad, factor_grad)
```

```python
import functools
import math

import jax
import jax.numpy as jnp
from jax import lax
from jax.experimental import pallas as pl
from jax.experimental.pallas import tpu as pltpu
from jax.sharding import PartitionSpec as P

MESH = pl.DeviceIdType.MESH
F32 = jnp.float32
BF16 = jnp.bfloat16


def two_factors(n):
    fast = max(d for d in range(1, n + 1) if n % d == 0 and d * d <= n)
    return n // fast, fast


def split(x):
    hi = x.astype(BF16)
    return hi, (x - hi.astype(F32)).astype(BF16)


def dot3(left, right, dims):
    one = functools.partial(lax.dot_general, dimension_numbers=(dims, ((), ())), preferred_element_type=F32)
    return one(left[0], right[0]) + (one(left[0], right[1]) + one(left[1], right[0]))


def kernel(cfg, x_ref, core_ref, chol_ref, res_ref, cg_ref, fg_ref,
           xpad, xhi, xlo, x8, x8b, vhi, vlo, fit, rec_y, sum_y, rec_z, cbuf, resid, outer, cg, cols,
           cg_core, cg_half, cg_row, cg_fin, inner, inner_rec,
           x8_s, x8_r, c_s, c_r, y_s, y_r, z_s, z_r, gz_s, gz_r, gy_s, gy_r, p_s, p_r, i_s, i_r, k_s, k_r, h_s, h_r, f_s, f_r):
    nrow, slow, fast, npp, rows, rpad, vec, cg_scale, fg_scale = cfg
    ngrid = slow * fast
    np_all = npp * ngrid
    per_row = ngrid // nrow
    pts = x_ref.shape[1]
    half = pts // 2
    r = lax.axis_index("row")
    j = lax.axis_index("grid")
    a = j // fast
    b = j % fast
    owner = j // per_row

    def remote(src, dst, ssem, rsem, **device):
        return pltpu.make_async_remote_copy(src_ref=src, dst_ref=dst, send_sem=ssem, recv_sem=rsem, device_id=device, device_id_type=MESH)

    barrier = pltpu.get_barrier_semaphore()
    for e in range(1, nrow):
        pl.semaphore_signal(barrier, inc=1, device_id={"row": (r + e) % nrow}, device_id_type=MESH)
    for e in range(1, ngrid):
        pl.semaphore_signal(barrier, inc=1, device_id={"grid": (j + e) % ngrid}, device_id_type=MESH)
    pl.semaphore_wait(barrier, nrow + ngrid - 2)

    def x8_copy(e):
        return remote(x8, x8, x8_s.at[e - 1], x8_r.at[0], row=(r + e) % nrow)

    def c_copy(e):
        to = (r + e) % nrow
        return remote(chol_ref.at[to], cbuf, c_s.at[e - 1], c_r.at[0], row=to)

    @pl.when(r == 0)
    def _():
        x8[...] = x_ref[0:np_all, :]
        for e in range(1, nrow):
            x8_copy(e).start()

    @pl.when(r == owner)
    def _():
        for e in range(1, nrow):
            c_copy(e).start()
        cbuf[...] = chol_ref[r]

    xpad[rpad - 16:rpad, :] = jnp.zeros((16, pts), F32)
    xpad[0:rows, :] = x_ref[...]
    hi, lo = split(xpad[...])
    xhi[...] = hi
    xlo[...] = lo

    @pl.when(r != 0)
    def _():
        x8_copy(1).wait_recv()

    flip = jnp.transpose(jnp.concatenate([x8[...], jnp.zeros((vec - np_all, pts), F32)], axis=0))
    for p in range(np_all):
        x8b[p] = jnp.broadcast_to(flip[:, p:p + 1], (pts, vec))

    def y_copy(d, e):
        to = (b + e) % fast
        group = (a + d) % slow
        return remote(fit.at[group * fast + to], rec_y.at[e - 1, d - 1], y_s.at[e - 1, d - 1], y_r.at[e - 1, d - 1], grid=a * fast + to)

    width = fast * npp * vec
    for d in range(1, slow + 1):
        group = (a + d) % slow
        for i in range(fast * npp):
            hi, lo = split(x8b[group * (fast * npp) + i] * core_ref[...])
            vhi[group, :, i * vec:(i + 1) * vec] = hi
            vlo[group, :, i * vec:(i + 1) * vec] = lo
        part = dot3((xhi[...], xlo[...]), (vhi[group], vlo[group]), ((1,), (0,)))
        for i in range(fast * npp):
            fit[group * fast + i // npp, i % npp] = part[:, i * vec:(i + 1) * vec]
        for e in range(1, fast):
            y_copy(d, e).start()

    def z_copy(d):
        return remote(sum_y.at[d - 1], rec_z.at[d - 1], z_s.at[d - 1], z_r.at[d - 1], grid=((a + d) % slow) * fast + b)

    for d in range(1, slow + 1):
        group = (a + d) % slow
        acc = fit[group * fast + b]
        for e in range(1, fast):
            y_copy(d, e).wait_recv()
            acc = acc + rec_y[e - 1, d - 1]
        sum_y[d - 1] = acc
        if d < slow:
            z_copy(d).start()

    @pl.when(r != owner)
    def _():
        c_copy(1).wait_recv()

    acc = sum_y[slow - 1]
    for d in range(1, slow):
        z_copy(d).wait_recv()
        acc = acc + rec_z[d - 1]
    resid[j] = cbuf[...] - acc

    def gz_copy(d):
        return remote(resid.at[j], resid.at[j], gz_s.at[d - 1], gz_r.at[d - 1], grid=((a + d) % slow) * fast + b)

    def gy_copy(d, e):
        piece = ((a + slow - d) % slow) * fast + b
        return remote(resid.at[piece], resid.at[piece], gy_s.at[e - 1, d], gy_r.at[e - 1, d], grid=a * fast + (b + e) % fast)

    def p_copy(d, e):
        piece = ((a + slow - d) % slow) * fast + (b + fast - e) % fast
        keeps = piece // per_row
        return keeps, remote(resid.at[piece], res_ref.at[piece % per_row, r], p_s.at[d, e], p_r.at[piece % per_row, r], row=keeps), pltpu.make_async_copy(resid.at[piece], res_ref.at[piece % per_row, r], p_s.at[d, e])

    def to_keeper(d, e):
        keeps, far, near = p_copy(d, e)

        @pl.when(keeps != r)
        def _():
            far.start()

        @pl.when(keeps == r)
        def _():
            near.start()

    for d in range(1, slow):
        gz_copy(d).start()
    for e in range(1, fast):
        gy_copy(0, e).start()
    to_keeper(0, 0)

    outer[...] = jnp.zeros_like(outer)
    cg[...] = jnp.zeros_like(cg)
    cols[...] = jnp.zeros_like(cols)
    lane = lax.broadcasted_iota(jnp.int32, (pts, vec), 1)
    for d in range(slow):
        if d + 1 < slow:
            gz_copy(d + 1).wait_recv()
            for e in range(1, fast):
                gy_copy(d + 1, e).start()
            to_keeper(d + 1, 0)
        for e in range(1, fast):
            gy_copy(d, e).wait_recv()
            to_keeper(d, e)
        group = (a + slow - d) % slow
        parts = [resid[group * fast + i // npp, i % npp] for i in range(fast * npp)]
        rs = split(jnp.concatenate(parts, axis=1))
        outer[...] += dot3(rs, (vhi[group], vlo[group]), ((1,), (1,)))
        w = dot3((xhi[...], xlo[...]), rs, ((0,), (0,)))
        for i in range(fast * npp):
            p = group * (fast * npp) + i
            wp = w[:, i * vec:(i + 1) * vec]
            cg[...] += x8b[p] * wp
            cols[...] += jnp.where(lane == p, jnp.sum(wp * core_ref[...], axis=1, keepdims=True), 0.0)

    odd = r % 2
    mate = r + 1 - 2 * odd
    k_copy = remote(cg.at[pl.ds((1 - odd) * half, half)], cg_core, k_s.at[0], k_r.at[0], row=mate)
    k_copy.start()

    inner[...] = jnp.transpose(cols[...])[0:np_all, :]

    def i_copy():
        return remote(inner, inner_rec.at[r - 1], i_s.at[0], i_r.at[r - 1], row=0)

    @pl.when(r != 0)
    def _():
        i_copy().start()

    k_copy.wait_recv()
    cg_half[...] = cg[pl.ds(odd * half, half), :] + cg_core[...]

    def h_copy(t):
        return remote(cg_half, cg_row.at[t - 1], h_s.at[t - 1], h_r.at[t - 1], row=(r + 2 * t) % nrow)

    for t in range(1, nrow // 2):
        h_copy(t).start()

    fg_ref[...] = fg_scale * outer[0:rows, :]

    @pl.when(r == 0)
    def _():
        acc = outer[0:np_all, :] + inner[...]
        for e in range(1, nrow):
            remote(inner, inner_rec.at[e - 1], i_s.at[0], i_r.at[e - 1], row=e).wait_recv()
            acc = acc + inner_rec[e - 1]
        fg_ref[0:np_all, :] = fg_scale * acc

    acc = cg_half[...]
    for t in range(1, nrow // 2):
        h_copy(t).wait_recv()
        acc = acc + cg_row[t - 1]
    cg_fin[odd] = cg_scale * acc
    f_copy = remote(cg_fin.at[odd], cg_fin.at[odd], f_s.at[0], f_r.at[0], row=mate)
    f_copy.start()
    cg_ref[pl.ds(odd * half, half), :] = cg_fin[odd]
    f_copy.wait_recv()
    cg_ref[pl.ds((1 - odd) * half, half), :] = cg_fin[1 - odd]

    for t in range(per_row):
        for e in range(1, nrow):
            far = (r + e) % nrow
            remote(resid.at[0], res_ref.at[t, far], p_s.at[0, 0], p_r.at[t, far], row=far).wait_recv()
    for d in range(slow):
        for e in range(fast):
            keeps, far, near = p_copy(d, e)

            @pl.when(keeps != r)
            def _():
                far.wait_send()

            @pl.when(keeps == r)
            def _():
                near.wait()

    @pl.when(r == 0)
    def _():
        for e in range(1, nrow):
            x8_copy(e).wait_send()

    @pl.when(r == owner)
    def _():
        for e in range(1, nrow):
            c_copy(e).wait_send()

    @pl.when(r != 0)
    def _():
        i_copy().wait_send()

    for e in range(1, fast):
        for d in range(slow):
            y_copy(d + 1, e).wait_send()
            gy_copy(d, e).wait_send()
    for d in range(1, slow):
        z_copy(d).wait_send()
        gz_copy(d).wait_send()
    for t in range(1, nrow // 2):
        h_copy(t).wait_send()
    k_copy.wait_send()
    f_copy.wait_send()


def per_device(nrow, ngrid, cholesky, factor, core):
    held = cholesky.shape[0]
    rows, pts = factor.shape
    vec = core.shape[1]
    np_all = held * nrow
    npp = np_all // ngrid
    per_row = held // npp
    slow, fast = two_factors(ngrid)
    rpad = -(-rows // 16) * 16
    cg_scale = -1.0 / math.sqrt(np_all * rows * nrow)
    fg_scale = -math.sqrt(pts * ngrid / (rows * nrow * vec))
    cfg = (nrow, slow, fast, npp, rows, rpad, vec, cg_scale, fg_scale)

    slab = cholesky.reshape(held, nrow, rows, vec)
    slab = lax.dynamic_slice_in_dim(slab, (lax.axis_index("grid") % per_row) * npp, npp, 0)
    slab = jnp.pad(jnp.swapaxes(slab, 0, 1), ((0, 0), (0, 0), (0, rpad - rows), (0, 0)))

    piece = (npp, rpad, vec)
    dma = pltpu.SemaphoreType.DMA
    vmem = pl.BlockSpec(memory_space=pltpu.VMEM)
    width = fast * npp * vec
    scratch = [
        pltpu.VMEM((rpad, pts), F32), pltpu.VMEM((rpad, pts), BF16), pltpu.VMEM((rpad, pts), BF16),
        pltpu.VMEM((np_all, pts), F32), pltpu.VMEM((np_all, pts, vec), F32),
        pltpu.VMEM((slow, pts, width), BF16), pltpu.VMEM((slow, pts, width), BF16),
        pltpu.VMEM((ngrid,) + piece, F32),
        pltpu.VMEM((max(fast - 1, 1), slow) + piece, F32), pltpu.VMEM((slow,) + piece, F32),
        pltpu.VMEM((max(slow - 1, 1),) + piece, F32), pltpu.VMEM(piece, F32),
        pltpu.VMEM((ngrid,) + piece, F32),
        pltpu.VMEM((rpad, pts), F32), pltpu.VMEM((pts, vec), F32), pltpu.VMEM((pts, vec), F32),
        pltpu.VMEM((pts // 2, vec), F32), pltpu.VMEM((pts // 2, vec), F32),
        pltpu.VMEM((max(nrow // 2 - 1, 1), pts // 2, vec), F32), pltpu.VMEM((2, pts // 2, vec), F32),
        pltpu.VMEM((np_all, pts), F32), pltpu.VMEM((nrow - 1, np_all, pts), F32),
        dma((nrow - 1,)), dma((1,)), dma((nrow - 1,)), dma((1,)),
        dma((max(fast - 1, 1), slow)), dma((max(fast - 1, 1), slow)), dma((max(slow - 1, 1),)), dma((max(slow - 1, 1),)),
        dma((max(slow - 1, 1),)), dma((max(slow - 1, 1),)), dma((max(fast - 1, 1), slow)), dma((max(fast - 1, 1), slow)),
        dma((slow, fast)), dma((per_row, nrow)), dma((1,)), dma((nrow - 1,)),
        dma((1,)), dma((1,)), dma((max(nrow // 2 - 1, 1),)), dma((max(nrow // 2 - 1, 1),)), dma((1,)), dma((1,)),
    ]
    macs = 3 * rows * pts * np_all * vec
    res, cg, fg = pl.pallas_call(
        functools.partial(kernel, cfg),
        out_shape=(
            jax.ShapeDtypeStruct((per_row, nrow) + piece, F32),
            jax.ShapeDtypeStruct((pts, vec), F32),
            jax.ShapeDtypeStruct((rows, pts), F32),
        ),
        in_specs=[vmem] * 3,
        out_specs=(pl.BlockSpec(memory_space=pl.ANY), vmem, vmem),
        scratch_shapes=scratch,
        cost_estimate=pl.CostEstimate(flops=6 * macs, bytes_accessed=8 * rows * pts, transcendentals=0),
        compiler_params=pltpu.CompilerParams(collective_id=0, has_side_effects=True, vmem_limit_bytes=44 * 2**20),
        name="hypercontraction",
    )(factor, core, slab)
    res = jnp.swapaxes(res[:, :, :, :rows], 1, 2).reshape(held, nrow * rows * vec)
    return res, cg, fg


def solution(mesh):
    placed = (P("row", None), P("row", "grid"), P("grid", None))
    return jax.shard_map(
        functools.partial(per_device, mesh.shape["row"], mesh.shape["grid"]),
        mesh=mesh,
        in_specs=placed,
        out_specs=(P("row", None), P("grid", None), P("row", "grid")),
        check_vma=False,
    )
```

```python
import functools
import math

import jax
import jax.numpy as jnp
from jax import lax
from jax.experimental import pallas as pl
from jax.experimental.pallas import tpu as pltpu
from jax.sharding import PartitionSpec as P

MESH = pl.DeviceIdType.MESH
F32 = jnp.float32
BF16 = jnp.bfloat16


def split(x):
    hi = x.astype(BF16)
    return hi, (x - hi.astype(F32)).astype(BF16)


def dot3(left, right, dims):
    one = functools.partial(lax.dot_general, dimension_numbers=(dims, ((), ())), preferred_element_type=F32)
    return one(left[0], right[0]) + (one(left[0], right[1]) + one(left[1], right[0]))


def low_bit(m, bits):
    return next((s for s in range(bits) if m >> s & 1), bits)


def mirrored(m, bits):
    return sum((m >> s & 1) << (bits - 1 - s) for s in range(bits))


def kernel(cfg, x_hbm, core_hbm, chol_hbm, res_ref, cg_ref, fg_ref,
           xraw, xpad, core_ref, chol, xhi, xlo, x8, x8b, vhi, vlo, fit, rec, csend, cbuf, resid, prec, outer, cg, cols,
           cg_core, cg_half, cg_row, cg_fin, inner, inner_rec,
           in_s, x8_s, x8_r, c_s, c_r, rs_s, rs_r, ag_s, ag_r, p_s, p_r, i_s, i_r, k_s, k_r, h_s, h_r, f_s, f_r):
    nrow, bits, npp, held, rows, rpad, vec, chunks, cg_scale, fg_scale = cfg
    ngrid = 1 << bits
    np_all = npp * ngrid
    per_row = held // npp
    pts = x_hbm.shape[1]
    half = pts // 2
    r = lax.axis_index("row")
    j = lax.axis_index("grid")
    flips = [(1 - 2 * ((j // (1 << s)) % 2)) * (1 << s) for s in range(bits)]
    owner = j // per_row
    spans = [pl.ds(at, size) for at, size in chunks]

    def at(m):
        return j + sum(flips[s] for s in range(bits) if m >> s & 1)

    def remote(src, dst, ssem, rsem, **device):
        return pltpu.make_async_remote_copy(src_ref=src, dst_ref=dst, send_sem=ssem, recv_sem=rsem, device_id=device, device_id_type=MESH)

    x_in = pltpu.make_async_copy(x_hbm, xraw, in_s.at[0])
    core_in = pltpu.make_async_copy(core_hbm, core_ref, in_s.at[1])
    chol_in = pltpu.make_async_copy(chol_hbm, chol, in_s.at[2])
    x_in.start()
    core_in.start()
    chol_in.start()

    barrier = pltpu.get_barrier_semaphore()
    for e in range(1, nrow):
        pl.semaphore_signal(barrier, inc=1, device_id={"row": (r + e) % nrow}, device_id_type=MESH)
    for s in range(bits):
        pl.semaphore_signal(barrier, inc=1, device_id={"grid": at(1 << s)}, device_id_type=MESH)
    x_in.wait()
    pl.semaphore_wait(barrier, nrow - 1 + bits)

    def x8_copy(e):
        return remote(x8, x8, x8_s.at[e - 1], x8_r.at[0], row=(r + e) % nrow)

    def c_copy(e):
        to = (r + e) % nrow
        return remote(csend.at[to], cbuf, c_s.at[e - 1], c_r.at[0], row=to)

    @pl.when(r == 0)
    def _():
        x8[...] = xraw[0:np_all, :]
        for e in range(1, nrow):
            x8_copy(e).start()

    if rpad > rows:
        xpad[rows:rpad, :] = jnp.zeros((rpad - rows, pts), F32)
    xpad[0:rows, :] = xraw[...]
    hi, lo = split(xpad[...])
    xhi[...] = hi
    xlo[...] = lo
    chol_in.wait()
    for t in range(per_row):
        @pl.when((r == owner) & (j % per_row == t))
        def _():
            for to in range(nrow):
                for i in range(npp):
                    if rpad > rows:
                        csend[to, i, rows:rpad, :] = jnp.zeros((rpad - rows, vec), F32)
                    csend[to, i, 0:rows, :] = chol[pl.ds(to * rows * held + t * npp + i, rows, stride=held), :]

    @pl.when(r == owner)
    def _():
        for e in range(1, nrow):
            c_copy(e).start()
        cbuf[...] = csend[r]

    core_in.wait()

    @pl.when(r != 0)
    def _():
        x8_copy(1).wait_recv()

    flip = jnp.transpose(jnp.concatenate([x8[...], jnp.zeros((vec - np_all, pts), F32)], axis=0))
    for p in range(np_all):
        x8b[p] = jnp.broadcast_to(flip[:, p:p + 1], (pts, vec))

    slots = {}
    for s in range(bits):
        for m in range(0, ngrid, 2 << s):
            slots[s, m] = len(slots)

    def rs_copy(c, s, m):
        slot = slots[s, m ^ 1 << s]
        return remote(fit.at[at(m), :, spans[c]], rec.at[slot, :, spans[c]], rs_s.at[c, slot], rs_r.at[c, slot], grid=at(1 << s))

    down = sorted(range(ngrid), key=lambda m: -mirrored(m, bits))
    up = down[::-1]
    width = npp * vec
    for c, span in enumerate(spans):
        for first in range(0, ngrid, 2):
            two = down[first:first + 2]
            if c == 0:
                for m in two:
                    for i in range(npp):
                        hi, lo = split(x8b[at(m) * npp + i] * core_ref[...])
                        vhi[at(m), :, i * vec:(i + 1) * vec] = hi
                        vlo[at(m), :, i * vec:(i + 1) * vec] = lo
            v = [jnp.concatenate([buf[at(m)] for m in two], axis=1) for buf in (vhi, vlo)]
            part = dot3((xhi[span, :], xlo[span, :]), v, ((1,), (0,)))
            for n, m in enumerate(two):
                for i in range(npp):
                    fit[at(m), i, span, :] = part[:, n * width + i * vec:n * width + (i + 1) * vec]
                if m % 2:
                    rs_copy(c, 0, m).start()

    def ag_copy(c, s, m):
        return remote(resid.at[at(m), :, spans[c]], resid.at[at(m), :, spans[c]], ag_s.at[c, m + (1 << s)], ag_r.at[c, m + (1 << s)], grid=at(1 << s))

    def ag_wait(c, m):
        s = low_bit(m, bits)
        remote(resid.at[at(m), :, spans[c]], resid.at[at(m), :, spans[c]], ag_s.at[c, m], ag_r.at[c, m], grid=at(1 << s)).wait_recv()

    def p_copy(c, m):
        piece = at(m)
        keeps = piece // per_row
        src, dst = resid.at[piece, :, spans[c]], prec.at[piece % per_row, r, :, spans[c]]
        return keeps, remote(src, dst, p_s.at[c, m], p_r.at[c, piece % per_row, r], row=keeps), pltpu.make_async_copy(src, dst, p_s.at[c, m])

    def pass_on(c, m):
        for s in reversed(range(low_bit(m, bits))):
            ag_copy(c, s, m).start()
        keeps, far, near = p_copy(c, m)

        @pl.when(keeps != r)
        def _():
            far.start()

        @pl.when(keeps == r)
        def _():
            near.start()

    def reduce(c, m):
        for s in range(low_bit(m, bits)):
            rs_copy(c, s, m | 1 << s).wait_recv()
            fit[at(m), :, spans[c], :] += rec[slots[s, m], :, spans[c], :]
        if m:
            rs_copy(c, low_bit(m, bits), m).start()
            return
        if c == 0:
            @pl.when(r != owner)
            def _():
                c_copy(1).wait_recv()
        resid[j, :, spans[c], :] = cbuf[:, spans[c], :] - fit[j, :, spans[c], :]
        pass_on(c, 0)

    def arrive(c, m):
        ag_wait(c, m)
        pass_on(c, m)

    lane = lax.broadcasted_iota(jnp.int32, (pts, vec), 1)

    def gradient(c, first):
        two = up[first:first + 2]
        span = spans[c]
        rs = split(jnp.concatenate([resid[at(m), i, span, :] for m in two for i in range(npp)], axis=1))
        v = [jnp.concatenate([buf[at(m)] for m in two], axis=1) for buf in (vhi, vlo)]
        out = dot3(rs, v, ((1,), (1,)))
        outer[span, :] = out if first == 0 else outer[span, :] + out
        w = dot3((xhi[span, :], xlo[span, :]), rs, ((0,), (0,)))
        add_cg, add_cols = None, None
        for n, m in enumerate(two):
            for i in range(npp):
                p = at(m) * npp + i
                wp = w[:, n * width + i * vec:n * width + (i + 1) * vec]
                one = x8b[p] * wp
                col = jnp.where(lane == p, jnp.sum(wp * core_ref[...], axis=1, keepdims=True), 0.0)
                add_cg = one if add_cg is None else add_cg + one
                add_cols = col if add_cols is None else add_cols + col
        if c == 0 and first == 0:
            cg[...] = add_cg
            cols[...] = add_cols
        else:
            cg[...] += add_cg
            cols[...] += add_cols

    evens = [m for m in down if m % 2 == 0]
    inner_up = [m for m in up if m and m % 2 == 0]
    last = len(spans) - 1
    for m in evens:
        reduce(0, m)
    for c in range(1, last + 1):
        todo = list(inner_up)
        for n, m in enumerate(evens):
            reduce(c, m)
            if n >= len(evens) // 2 - 1 and m:
                for _ in range(2 if n == len(evens) // 2 - 1 else 1):
                    if todo:
                        arrive(c - 1, todo.pop(0))
        for m in todo:
            arrive(c - 1, m)
        odd_up = [m for m in up if m % 2]
        for n, m in enumerate(odd_up):
            arrive(c - 1, m)
            if n == len(odd_up) // 2 - 1:
                gradient(c - 1, 0)
        if c < last:
            for first in range(2, ngrid, 2):
                gradient(c - 1, first)
    pending = [(last - 1, first) for first in range(2, ngrid, 2)] if last else []
    for m in inner_up:
        arrive(last, m)
        if pending:
            gradient(*pending.pop(0))
    while pending:
        gradient(*pending.pop(0))
    for first in range(0, ngrid // 2, 2):
        gradient(last, first)
    for first in range(ngrid // 2, ngrid, 2):
        for m in up[first:first + 2]:
            arrive(last, m)
        gradient(last, first)

    odd = r % 2
    mate = r + 1 - 2 * odd
    k_copy = remote(cg.at[pl.ds((1 - odd) * half, half)], cg_core, k_s.at[0], k_r.at[0], row=mate)
    k_copy.start()

    inner[...] = jnp.transpose(cols[...])[0:np_all, :]

    def i_copy():
        return remote(inner, inner_rec.at[r - 1], i_s.at[0], i_r.at[r - 1], row=0)

    @pl.when(r != 0)
    def _():
        i_copy().start()

    k_copy.wait_recv()
    cg_half[...] = cg[pl.ds(odd * half, half), :] + cg_core[...]

    def h_copy(t):
        return remote(cg_half, cg_row.at[t - 1], h_s.at[t - 1], h_r.at[t - 1], row=(r + 2 * t) % nrow)

    for t in range(1, nrow // 2):
        h_copy(t).start()

    fg_ref[...] = fg_scale * outer[0:rows, :]

    @pl.when(r == 0)
    def _():
        acc = outer[0:np_all, :] + inner[...]
        for e in range(1, nrow):
            remote(inner, inner_rec.at[e - 1], i_s.at[0], i_r.at[e - 1], row=e).wait_recv()
            acc = acc + inner_rec[e - 1]
        fg_ref[0:np_all, :] = fg_scale * acc

    for c in range(len(spans)):
        for m in range(ngrid):
            keeps, far, near = p_copy(c, m)

            @pl.when(keeps != r)
            def _():
                far.wait_send()

            @pl.when(keeps == r)
            def _():
                near.wait()
    for src in range(nrow):
        @pl.when(r != src)
        def _():
            for t in range(per_row):
                for c, span in enumerate(spans):
                    here = prec.at[t, src, :, span]
                    remote(here, here, p_s.at[0, 0], p_r.at[c, t, src], row=src).wait_recv()

        for t in range(per_row):
            for i in range(npp):
                res_ref[pl.ds(src * rows * held + t * npp + i, rows, stride=held), :] = prec[t, src, i, 0:rows, :]

    acc = cg_half[...]
    for t in range(1, nrow // 2):
        h_copy(t).wait_recv()
        acc = acc + cg_row[t - 1]
    cg_fin[odd] = cg_scale * acc
    f_copy = remote(cg_fin.at[odd], cg_fin.at[odd], f_s.at[0], f_r.at[0], row=mate)
    f_copy.start()
    cg_ref[pl.ds(odd * half, half), :] = cg_fin[odd]
    f_copy.wait_recv()
    cg_ref[pl.ds((1 - odd) * half, half), :] = cg_fin[1 - odd]

    @pl.when(r == 0)
    def _():
        for e in range(1, nrow):
            x8_copy(e).wait_send()

    @pl.when(r == owner)
    def _():
        for e in range(1, nrow):
            c_copy(e).wait_send()

    @pl.when(r != 0)
    def _():
        i_copy().wait_send()

    for c in range(len(spans)):
        for s in range(bits):
            for m in range(0, ngrid, 2 << s):
                rs_copy(c, s, m | 1 << s).wait_send()
                ag_copy(c, s, m).wait_send()
    for t in range(1, nrow // 2):
        h_copy(t).wait_send()
    k_copy.wait_send()
    f_copy.wait_send()


def per_device(nrow, ngrid, cholesky, factor, core):
    held = cholesky.shape[0]
    rows, pts = factor.shape
    vec = core.shape[1]
    np_all = held * nrow
    npp = np_all // ngrid
    per_row = held // npp
    bits = ngrid.bit_length() - 1
    rpad = -(-rows // 16) * 16
    size = -(-rpad // 32) * 16
    chunks = [(0, size), (size, rpad - size)]
    cg_scale = -1.0 / math.sqrt(np_all * rows * nrow)
    fg_scale = -math.sqrt(pts * ngrid / (rows * nrow * vec))
    cfg = (nrow, bits, npp, held, rows, rpad, vec, chunks, cg_scale, fg_scale)

    slab = jnp.swapaxes(cholesky.reshape(held, nrow * rows, vec), 0, 1).reshape(nrow * rows * held, vec)

    piece = (npp, rpad, vec)
    nc = len(chunks)
    dma = pltpu.SemaphoreType.DMA
    vmem = pl.BlockSpec(memory_space=pltpu.VMEM)
    hbm = pl.BlockSpec(memory_space=pltpu.HBM)
    f32 = lambda *shape: pltpu.VMEM(shape, F32)
    b16 = lambda *shape: pltpu.VMEM(shape, BF16)
    pairs = max(nrow // 2 - 1, 1)
    scratch = [
        f32(rows, pts), f32(rpad, pts), f32(pts, vec), f32(nrow * rows * held, vec), b16(rpad, pts), b16(rpad, pts),
        f32(np_all, pts), f32(np_all, pts, vec),
        b16(ngrid, pts, npp * vec), b16(ngrid, pts, npp * vec),
        f32(ngrid, *piece), f32(ngrid - 1, *piece), f32(nrow, *piece), f32(*piece),
        f32(ngrid, *piece), f32(per_row, nrow, *piece),
        f32(rpad, pts), f32(pts, vec), f32(pts, vec),
        f32(pts // 2, vec), f32(pts // 2, vec), f32(pairs, pts // 2, vec), f32(2, pts // 2, vec),
        f32(np_all, pts), f32(nrow - 1, np_all, pts),
        dma((3,)), dma((nrow - 1,)), dma((1,)), dma((nrow - 1,)), dma((1,)),
        dma((nc, ngrid - 1)), dma((nc, ngrid - 1)), dma((nc, ngrid)), dma((nc, ngrid)),
        dma((nc, ngrid)), dma((nc, per_row, nrow)), dma((1,)), dma((nrow - 1,)),
        dma((1,)), dma((1,)), dma((pairs,)), dma((pairs,)), dma((1,)), dma((1,)),
    ]
    macs = 3 * rows * pts * np_all * vec
    res, cg, fg = pl.pallas_call(
        functools.partial(kernel, cfg),
        out_shape=(
            jax.ShapeDtypeStruct((nrow * rows * held, vec), F32),
            jax.ShapeDtypeStruct((pts, vec), F32),
            jax.ShapeDtypeStruct((rows, pts), F32),
        ),
        in_specs=[hbm] * 3,
        out_specs=(vmem, vmem, vmem),
        scratch_shapes=scratch,
        cost_estimate=pl.CostEstimate(flops=6 * macs, bytes_accessed=8 * rows * pts, transcendentals=0),
        compiler_params=pltpu.CompilerParams(collective_id=0, has_side_effects=True, vmem_limit_bytes=48 * 2**20),
        name="hypercontraction",
    )(factor, core, slab)
    res = jnp.swapaxes(res.reshape(nrow * rows, held, vec), 0, 1).reshape(held, nrow * rows * vec)
    return res, cg, fg


def solution(mesh):
    placed = (P("row", None), P("row", "grid"), P("grid", None))
    return jax.shard_map(
        functools.partial(per_device, mesh.shape["row"], mesh.shape["grid"]),
        mesh=mesh,
        in_specs=placed,
        out_specs=(P("row", None), P("grid", None), P("row", "grid")),
        check_vma=False,
    )
```

```python
import functools
import math

import jax
import jax.numpy as jnp
from jax import lax
from jax.experimental import pallas as pl
from jax.experimental.pallas import tpu as pltpu
from jax.sharding import PartitionSpec as P

MESH = pl.DeviceIdType.MESH
F32 = jnp.float32
BF16 = jnp.bfloat16


def split(x):
    hi = x.astype(BF16)
    return hi, (x - hi.astype(F32)).astype(BF16)


def dot3(left, right, dims):
    one = functools.partial(lax.dot_general, dimension_numbers=(dims, ((), ())), preferred_element_type=F32)
    return one(left[0], right[0]) + (one(left[0], right[1]) + one(left[1], right[0]))


def low_bit(m, bits):
    return next((s for s in range(bits) if m >> s & 1), bits)


def mirrored(m, bits):
    return sum((m >> s & 1) << (bits - 1 - s) for s in range(bits))


def kernel(cfg, x_hbm, core_hbm, chol_hbm, res_hbm, cg_hbm, fg_hbm,
           xraw, xpad, core_ref, chol, xhi, xlo, x8, x8b, vhi, vlo, core_t, thi, tlo, fit, rec, csend, cbuf, resid, prec, outer, cg_t, cg,
           res_ref, cg_ref, fg_ref,
           cg_core, cg_half, cg_row, cg_fin, inner, inner_rec,
           in_s, out_s, x8_s, x8_r, c_s, c_r, rs_s, rs_r, ag_s, ag_r, p_s, p_r, i_s, i_r, k_s, k_r, h_s, h_r, f_s, f_r):
    nrow, bits, npp, held, rows, rpad, vec, chunks, cg_scale, fg_scale = cfg
    ngrid = 1 << bits
    np_all = npp * ngrid
    per_row = held // npp
    pts = x_hbm.shape[1]
    half = pts // 2
    r = lax.axis_index("row")
    j = lax.axis_index("grid")
    flips = [(1 - 2 * ((j // (1 << s)) % 2)) * (1 << s) for s in range(bits)]
    owner = j // per_row
    spans = [pl.ds(at, size) for at, size in chunks]

    def at(m):
        return j + sum(flips[s] for s in range(bits) if m >> s & 1)

    def remote(src, dst, ssem, rsem, **device):
        return pltpu.make_async_remote_copy(src_ref=src, dst_ref=dst, send_sem=ssem, recv_sem=rsem, device_id=device, device_id_type=MESH)

    x_in = pltpu.make_async_copy(x_hbm, xraw, in_s.at[0])
    core_in = pltpu.make_async_copy(core_hbm, core_ref, in_s.at[1])
    chol_in = pltpu.make_async_copy(chol_hbm, chol, in_s.at[2])
    x_in.start()
    core_in.start()
    chol_in.start()

    barrier = pltpu.get_barrier_semaphore()
    for e in range(1, nrow):
        pl.semaphore_signal(barrier, inc=1, device_id={"row": (r + e) % nrow}, device_id_type=MESH)
    for s in range(bits):
        pl.semaphore_signal(barrier, inc=1, device_id={"grid": at(1 << s)}, device_id_type=MESH)
    x_in.wait()
    pl.semaphore_wait(barrier, nrow - 1 + bits)

    def x8_copy(e):
        return remote(x8, x8, x8_s.at[e - 1], x8_r.at[0], row=(r + e) % nrow)

    def c_copy(e):
        to = (r + e) % nrow
        return remote(csend.at[to], cbuf, c_s.at[e - 1], c_r.at[0], row=to)

    @pl.when(r == 0)
    def _():
        x8[...] = xraw[0:np_all, :]
        for e in range(1, nrow):
            x8_copy(e).start()

    if rpad > rows:
        xpad[rows:rpad, :] = jnp.zeros((rpad - rows, pts), F32)
    xpad[0:rows, :] = xraw[...]
    hi, lo = split(xpad[...])
    xhi[...] = hi
    xlo[...] = lo
    chol_in.wait()
    for t in range(per_row):
        @pl.when((r == owner) & (j % per_row == t))
        def _():
            for to in range(nrow):
                for i in range(npp):
                    if rpad > rows:
                        csend[to, i, rows:rpad, :] = jnp.zeros((rpad - rows, vec), F32)
                    csend[to, i, 0:rows, :] = chol[pl.ds(to * rows * held + t * npp + i, rows, stride=held), :]

    @pl.when(r == owner)
    def _():
        for e in range(1, nrow):
            c_copy(e).start()
        cbuf[...] = csend[r]

    core_in.wait()

    @pl.when(r != 0)
    def _():
        x8_copy(1).wait_recv()

    flip = jnp.transpose(jnp.concatenate([x8[...], jnp.zeros((vec - np_all, pts), F32)], axis=0))
    for p in range(np_all):
        x8b[p] = jnp.broadcast_to(flip[:, p:p + 1], (pts, vec))

    slots = {}
    for s in range(bits):
        for m in range(0, ngrid, 2 << s):
            slots[s, m] = len(slots)

    def rs_copy(c, s, m):
        slot = slots[s, m ^ 1 << s]
        return remote(fit.at[at(m), :, spans[c]], rec.at[slot, :, spans[c]], rs_s.at[c, slot], rs_r.at[c, slot], grid=at(1 << s))

    down = sorted(range(ngrid), key=lambda m: -mirrored(m, bits))
    up = down[::-1]
    width = npp * vec

    def partial_fit(c, first):
        span = spans[c]
        two = down[first:first + 2]
        if c == 0:
            for m in two:
                for i in range(npp):
                    hi, lo = split(x8b[at(m) * npp + i] * core_ref[...])
                    vhi[at(m), :, i * vec:(i + 1) * vec] = hi
                    vlo[at(m), :, i * vec:(i + 1) * vec] = lo
        v = [jnp.concatenate([buf[at(m)] for m in two], axis=1) for buf in (vhi, vlo)]
        part = dot3((xhi[span, :], xlo[span, :]), v, ((1,), (0,)))
        for n, m in enumerate(two):
            for i in range(npp):
                fit[at(m), i, span, :] = part[:, n * width + i * vec:n * width + (i + 1) * vec]
            if m % 2:
                rs_copy(c, 0, m).start()

    def ag_copy(c, s, m):
        return remote(resid.at[at(m), :, spans[c]], resid.at[at(m), :, spans[c]], ag_s.at[c, m + (1 << s)], ag_r.at[c, m + (1 << s)], grid=at(1 << s))

    def ag_wait(c, m):
        s = low_bit(m, bits)
        remote(resid.at[at(m), :, spans[c]], resid.at[at(m), :, spans[c]], ag_s.at[c, m], ag_r.at[c, m], grid=at(1 << s)).wait_recv()

    def p_copy(c, m):
        piece = at(m)
        keeps = piece // per_row
        src, dst = resid.at[piece, :, spans[c]], prec.at[piece % per_row, r, :, spans[c]]
        return keeps, remote(src, dst, p_s.at[c, m], p_r.at[c, piece % per_row, r], row=keeps), pltpu.make_async_copy(src, dst, p_s.at[c, m])

    def pass_on(c, m):
        for s in reversed(range(low_bit(m, bits))):
            ag_copy(c, s, m).start()
        keeps, far, near = p_copy(c, m)

        @pl.when(keeps != r)
        def _():
            far.start()

        @pl.when(keeps == r)
        def _():
            near.start()

    def reduce(c, m):
        for s in range(low_bit(m, bits)):
            rs_copy(c, s, m | 1 << s).wait_recv()
            fit[at(m), :, spans[c], :] += rec[slots[s, m], :, spans[c], :]
        if m:
            rs_copy(c, low_bit(m, bits), m).start()
            return
        if c == 0:
            @pl.when(r != owner)
            def _():
                c_copy(1).wait_recv()
        resid[j, :, spans[c], :] = cbuf[:, spans[c], :] - fit[j, :, spans[c], :]
        pass_on(c, 0)

    def arrive(c, m):
        ag_wait(c, m)
        pass_on(c, m)

    def gradient(c, first):
        two = up[first:first + 2]
        span = spans[c]
        piece = jnp.concatenate([resid[at(m), i, span, :] for m in two for i in range(npp)], axis=1)
        t = [jnp.concatenate([buf[at(m)] for m in two], axis=0) for buf in (thi, tlo)]
        out = dot3(split(piece), t, ((1,), (0,)))
        outer[span, :] = out if first == 0 else outer[span, :] + out
        w = dot3(split(jnp.transpose(piece)), (xhi[span, :], xlo[span, :]), ((1,), (0,)))
        more = None
        for n, m in enumerate(two):
            for i in range(npp):
                p = at(m) * npp + i
                wp = w[n * width + i * vec:n * width + (i + 1) * vec, :]
                one = x8[pl.ds(p, 1), :] * wp
                more = one if more is None else more + one
                row = jnp.sum(wp * core_t[...], axis=0, keepdims=True)
                inner[pl.ds(p, 1), :] = row if c == 0 else inner[pl.ds(p, 1), :] + row
        cg_t[...] = more if c == 0 and first == 0 else cg_t[...] + more

    evens = [m for m in down if m % 2 == 0]
    inner_up = [m for m in up if m and m % 2 == 0]
    last = len(spans) - 1
    for first in range(0, ngrid, 2):
        partial_fit(0, first)
    for c in range(1, last + 1):
        for first in range(0, ngrid // 2, 2):
            partial_fit(c, first)
    for m in evens[:len(evens) // 2]:
        reduce(0, m)
    for c in range(1, last + 1):
        for first in range(ngrid // 2, ngrid, 2):
            partial_fit(c, first)
    for m in evens[len(evens) // 2:-1]:
        reduce(0, m)
    core_t[...] = jnp.transpose(core_ref[...])
    for p in range(np_all):
        hi, lo = split(x8[p:p + 1, :] * core_t[...])
        thi[p // npp, p % npp * vec:(p % npp + 1) * vec, :] = hi
        tlo[p // npp, p % npp * vec:(p % npp + 1) * vec, :] = lo
    reduce(0, 0)
    for c in range(1, last + 1):
        todo = list(inner_up)
        for n, m in enumerate(evens):
            reduce(c, m)
            if n >= len(evens) // 2 - 1 and m:
                for _ in range(2 if n == len(evens) // 2 - 1 else 1):
                    if todo:
                        arrive(c - 1, todo.pop(0))
        for m in todo:
            arrive(c - 1, m)
        odd_up = [m for m in up if m % 2]
        for n, m in enumerate(odd_up):
            arrive(c - 1, m)
            if n == len(odd_up) // 2 - 1:
                gradient(c - 1, 0)
        if c < last:
            for first in range(2, ngrid, 2):
                gradient(c - 1, first)
    pending = [(last - 1, first) for first in range(2, ngrid, 2)] if last else []
    for m in inner_up:
        arrive(last, m)
        if pending:
            gradient(*pending.pop(0))
    while pending:
        gradient(*pending.pop(0))
    for first in range(0, ngrid // 2, 2):
        gradient(last, first)
    for first in range(ngrid // 2, ngrid, 2):
        for m in up[first:first + 2]:
            arrive(last, m)
        gradient(last, first)

    odd = r % 2
    mate = r + 1 - 2 * odd
    cg[...] = jnp.transpose(cg_t[...])
    k_copy = remote(cg.at[pl.ds((1 - odd) * half, half)], cg_core, k_s.at[0], k_r.at[0], row=mate)
    k_copy.start()

    def i_copy():
        return remote(inner, inner_rec.at[r - 1], i_s.at[0], i_r.at[r - 1], row=0)

    @pl.when(r != 0)
    def _():
        i_copy().start()

    k_copy.wait_recv()
    cg_half[...] = cg[pl.ds(odd * half, half), :] + cg_core[...]

    def h_copy(t):
        return remote(cg_half, cg_row.at[t - 1], h_s.at[t - 1], h_r.at[t - 1], row=(r + 2 * t) % nrow)

    for t in range(1, nrow // 2):
        h_copy(t).start()

    fg_ref[...] = fg_scale * outer[0:rows, :]

    @pl.when(r == 0)
    def _():
        acc = outer[0:np_all, :] + inner[...]
        for e in range(1, nrow):
            remote(inner, inner_rec.at[e - 1], i_s.at[0], i_r.at[e - 1], row=e).wait_recv()
            acc = acc + inner_rec[e - 1]
        fg_ref[0:np_all, :] = fg_scale * acc

    fg_out = pltpu.make_async_copy(fg_ref, fg_hbm, out_s.at[1])
    fg_out.start()

    for c in range(len(spans)):
        for m in range(ngrid):
            keeps, far, near = p_copy(c, m)

            @pl.when(keeps != r)
            def _():
                far.wait_send()

            @pl.when(keeps == r)
            def _():
                near.wait()
    for src in range(nrow):
        @pl.when(r != src)
        def _():
            for t in range(per_row):
                for c, span in enumerate(spans):
                    here = prec.at[t, src, :, span]
                    remote(here, here, p_s.at[0, 0], p_r.at[c, t, src], row=src).wait_recv()

        for t in range(per_row):
            for i in range(npp):
                res_ref[pl.ds(src * rows * held + t * npp + i, rows, stride=held), :] = prec[t, src, i, 0:rows, :]

    res_out = pltpu.make_async_copy(res_ref, res_hbm, out_s.at[0])
    res_out.start()

    acc = cg_half[...]
    for t in range(1, nrow // 2):
        h_copy(t).wait_recv()
        acc = acc + cg_row[t - 1]
    cg_fin[odd] = cg_scale * acc
    f_copy = remote(cg_fin.at[odd], cg_fin.at[odd], f_s.at[0], f_r.at[0], row=mate)
    f_copy.start()
    cg_ref[pl.ds(odd * half, half), :] = cg_fin[odd]
    f_copy.wait_recv()
    cg_ref[pl.ds((1 - odd) * half, half), :] = cg_fin[1 - odd]
    cg_out = pltpu.make_async_copy(cg_ref, cg_hbm, out_s.at[2])
    cg_out.start()

    @pl.when(r == 0)
    def _():
        for e in range(1, nrow):
            x8_copy(e).wait_send()

    @pl.when(r == owner)
    def _():
        for e in range(1, nrow):
            c_copy(e).wait_send()

    @pl.when(r != 0)
    def _():
        i_copy().wait_send()

    for c in range(len(spans)):
        for s in range(bits):
            for m in range(0, ngrid, 2 << s):
                rs_copy(c, s, m | 1 << s).wait_send()
                ag_copy(c, s, m).wait_send()
    for t in range(1, nrow // 2):
        h_copy(t).wait_send()
    k_copy.wait_send()
    f_copy.wait_send()
    res_out.wait()
    fg_out.wait()
    cg_out.wait()


def hand_out(res_in, cg_in, fg_in, res_out, cg_out, fg_out, sems):
    size = res_in.shape[0] // 4
    copies = [pltpu.make_async_copy(src, dst, sems.at[n]) for n, (src, dst) in enumerate([(fg_in, fg_out), (cg_in, cg_out)])]
    for n in range(4):
        part = pl.ds(n * size, size)
        copies.append(pltpu.make_async_copy(res_in.at[part], res_out.at[part], sems.at[2 + n]))
    for copy in copies:
        copy.start()
    for copy in copies:
        copy.wait()


def per_device(nrow, ngrid, cholesky, factor, core):
    held = cholesky.shape[0]
    rows, pts = factor.shape
    vec = core.shape[1]
    np_all = held * nrow
    npp = np_all // ngrid
    per_row = held // npp
    bits = ngrid.bit_length() - 1
    rpad = -(-rows // 16) * 16
    size = -(-rpad // 32) * 16
    chunks = [(0, size), (size, rpad - size)]
    cg_scale = -1.0 / math.sqrt(np_all * rows * nrow)
    fg_scale = -math.sqrt(pts * ngrid / (rows * nrow * vec))
    cfg = (nrow, bits, npp, held, rows, rpad, vec, chunks, cg_scale, fg_scale)

    slab = jnp.swapaxes(cholesky.reshape(held, nrow * rows, vec), 0, 1).reshape(nrow * rows * held, vec)

    piece = (npp, rpad, vec)
    nc = len(chunks)
    dma = pltpu.SemaphoreType.DMA
    hbm = pl.BlockSpec(memory_space=pltpu.HBM)
    f32 = lambda *shape: pltpu.VMEM(shape, F32)
    b16 = lambda *shape: pltpu.VMEM(shape, BF16)
    pairs = max(nrow // 2 - 1, 1)
    scratch = [
        f32(rows, pts), f32(rpad, pts), f32(pts, vec), f32(nrow * rows * held, vec), b16(rpad, pts), b16(rpad, pts),
        f32(np_all, pts), f32(np_all, pts, vec),
        b16(ngrid, pts, npp * vec), b16(ngrid, pts, npp * vec),
        f32(vec, pts), b16(ngrid, npp * vec, pts), b16(ngrid, npp * vec, pts),
        f32(ngrid, *piece), f32(ngrid - 1, *piece), f32(nrow, *piece), f32(*piece),
        f32(ngrid, *piece), f32(per_row, nrow, *piece),
        f32(rpad, pts), f32(vec, pts), f32(pts, vec),
        f32(nrow * rows * held, vec), f32(pts, vec), f32(rows, pts),
        f32(pts // 2, vec), f32(pts // 2, vec), f32(pairs, pts // 2, vec), f32(2, pts // 2, vec),
        f32(np_all, pts), f32(nrow - 1, np_all, pts),
        dma((3,)), dma((3,)), dma((nrow - 1,)), dma((1,)), dma((nrow - 1,)), dma((1,)),
        dma((nc, ngrid - 1)), dma((nc, ngrid - 1)), dma((nc, ngrid)), dma((nc, ngrid)),
        dma((nc, ngrid)), dma((nc, per_row, nrow)), dma((1,)), dma((nrow - 1,)),
        dma((1,)), dma((1,)), dma((pairs,)), dma((pairs,)), dma((1,)), dma((1,)),
    ]
    macs = 3 * rows * pts * np_all * vec
    results = (
        jax.ShapeDtypeStruct((nrow * rows * held, vec), F32),
        jax.ShapeDtypeStruct((pts, vec), F32),
        jax.ShapeDtypeStruct((rows, pts), F32),
    )
    made = pl.pallas_call(
        functools.partial(kernel, cfg),
        out_shape=results,
        in_specs=[hbm] * 3,
        out_specs=(hbm, hbm, hbm),
        scratch_shapes=scratch,
        cost_estimate=pl.CostEstimate(flops=6 * macs, bytes_accessed=8 * rows * pts, transcendentals=0),
        compiler_params=pltpu.CompilerParams(collective_id=0, has_side_effects=True, vmem_limit_bytes=62 * 2**20),
        name="hypercontraction",
    )(factor, core, slab)
    res, cg, fg = pl.pallas_call(
        hand_out,
        out_shape=results,
        in_specs=[pl.BlockSpec(memory_space=pl.ANY)] * 3,
        out_specs=(hbm, hbm, hbm),
        scratch_shapes=[dma((6,))],
        name="hand_out",
    )(*made)
    res = jnp.swapaxes(res.reshape(nrow * rows, held, vec), 0, 1).reshape(held, nrow * rows * vec)
    return res, cg, fg


def solution(mesh):
    placed = (P("row", None), P("row", "grid"), P("grid", None))
    return jax.shard_map(
        functools.partial(per_device, mesh.shape["row"], mesh.shape["grid"]),
        mesh=mesh,
        in_specs=placed,
        out_specs=(P("row", None), P("grid", None), P("row", "grid")),
        check_vma=False,
    )
```

```python
import functools
import math

import jax
import jax.numpy as jnp
from jax import lax
from jax.experimental import pallas as pl
from jax.experimental.pallas import tpu as pltpu
from jax.sharding import PartitionSpec as P

MESH = pl.DeviceIdType.MESH
F32 = jnp.float32
BF16 = jnp.bfloat16


def split(x):
    hi = x.astype(BF16)
    return hi, (x - hi.astype(F32)).astype(BF16)


def dot3(left, right, dims):
    one = functools.partial(lax.dot_general, dimension_numbers=(dims, ((), ())), preferred_element_type=F32)
    return one(left[0], right[0]) + (one(left[0], right[1]) + one(left[1], right[0]))


def low_bit(m, bits):
    return next((s for s in range(bits) if m >> s & 1), bits)


def mirrored(m, bits):
    return sum((m >> s & 1) << (bits - 1 - s) for s in range(bits))


def kernel(cfg, x_hbm, core_hbm, chol_hbm, res_hbm, cg_hbm, fg_hbm,
           xraw, xpad, core_ref, chol, xhi, xlo, x8, x8b, vhi, vlo, core_t, thi, tlo, fit, rec, csend, cbuf, resid, prec, outer, cg_t, cg,
           res_ref, cg_ref, fg_ref,
           cg_core, cg_half, cg_row, cg_fin, inner, inner_rec,
           in_s, out_s, x8_s, x8_r, c_s, c_r, rs_s, rs_r, ag_s, ag_r, p_s, p_r, i_s, i_r, k_s, k_r, h_s, h_r, f_s, f_r):
    nrow, bits, npp, held, rows, rpad, vec, chunks, orders, cg_scale, fg_scale = cfg
    ngrid = 1 << bits
    np_all = npp * ngrid
    per_row = held // npp
    pts = x_hbm.shape[1]
    half = pts // 2
    r = lax.axis_index("row")
    j = lax.axis_index("grid")
    flips = [(1 - 2 * ((j // (1 << s)) % 2)) * (1 << s) for s in range(bits)]
    owner = j // per_row
    spans = [pl.ds(begin, size) for begin, size in chunks]
    regions = [spans[0], pl.ds(chunks[1][0], rpad - chunks[1][0])]

    def moved(c, m):
        return sum(1 << orders[c][s] for s in range(bits) if m >> s & 1)

    def at(c, m):
        return j + sum(flips[s] for s in range(bits) if moved(c, m) >> s & 1)

    def remote(src, dst, ssem, rsem, **device):
        return pltpu.make_async_remote_copy(src_ref=src, dst_ref=dst, send_sem=ssem, recv_sem=rsem, device_id=device, device_id_type=MESH)

    x_in = pltpu.make_async_copy(x_hbm, xraw, in_s.at[0])
    core_in = pltpu.make_async_copy(core_hbm, core_ref, in_s.at[1])
    chol_in = pltpu.make_async_copy(chol_hbm, chol, in_s.at[2])
    x_in.start()
    core_in.start()
    chol_in.start()

    barrier = pltpu.get_barrier_semaphore()
    for e in range(1, nrow):
        pl.semaphore_signal(barrier, inc=1, device_id={"row": (r + e) % nrow}, device_id_type=MESH)
    for s in range(bits):
        pl.semaphore_signal(barrier, inc=1, device_id={"grid": at(0, 1 << s)}, device_id_type=MESH)
    x_in.wait()
    pl.semaphore_wait(barrier, nrow - 1 + bits)

    def x8_copy(e):
        return remote(x8, x8, x8_s.at[e - 1], x8_r.at[0], row=(r + e) % nrow)

    def c_copy(e):
        to = (r + e) % nrow
        return remote(csend.at[to], cbuf, c_s.at[e - 1], c_r.at[0], row=to)

    @pl.when(r == 0)
    def _():
        x8[...] = xraw[0:np_all, :]
        for e in range(1, nrow):
            x8_copy(e).start()

    if rpad > rows:
        xpad[rows:rpad, :] = jnp.zeros((rpad - rows, pts), F32)
    xpad[0:rows, :] = xraw[...]
    hi, lo = split(xpad[...])
    xhi[...] = hi
    xlo[...] = lo
    chol_in.wait()
    for t in range(per_row):
        @pl.when((r == owner) & (j % per_row == t))
        def _():
            for to in range(nrow):
                for i in range(npp):
                    if rpad > rows:
                        csend[to, i, rows:rpad, :] = jnp.zeros((rpad - rows, vec), F32)
                    csend[to, i, 0:rows, :] = chol[pl.ds(to * rows * held + t * npp + i, rows, stride=held), :]

    @pl.when(r == owner)
    def _():
        for e in range(1, nrow):
            c_copy(e).start()
        cbuf[...] = csend[r]

    core_in.wait()

    @pl.when(r != 0)
    def _():
        x8_copy(1).wait_recv()

    flip = jnp.transpose(jnp.concatenate([x8[...], jnp.zeros((vec - np_all, pts), F32)], axis=0))
    for p in range(np_all):
        x8b[p] = jnp.broadcast_to(flip[:, p:p + 1], (pts, vec))

    slots = {}
    for s in range(bits):
        for m in range(0, ngrid, 2 << s):
            slots[s, m] = len(slots)

    def rs_copy(c, s, m):
        slot = slots[s, m ^ 1 << s]
        return remote(fit.at[at(c, m), :, spans[c]], rec.at[slot, :, spans[c]], rs_s.at[c, slot], rs_r.at[c, slot], grid=at(c, 1 << s))

    down = sorted(range(ngrid), key=lambda m: -mirrored(m, bits))
    up = down[::-1]
    width = npp * vec
    late = []
    for first in range(0, ngrid, 2):
        two = down[first:first + 2]
        for m in two:
            for i in range(npp):
                hi, lo = split(x8b[at(0, m) * npp + i] * core_ref[...])
                vhi[at(0, m), :, i * vec:(i + 1) * vec] = hi
                vlo[at(0, m), :, i * vec:(i + 1) * vec] = lo
        v = [jnp.concatenate([buf[at(0, m)] for m in two], axis=1) for buf in (vhi, vlo)]
        part = dot3((xhi[...], xlo[...]), v, ((1,), (0,)))
        for n, m in enumerate(two):
            for i in range(npp):
                fit[at(0, m), i] = part[:, n * width + i * vec:n * width + (i + 1) * vec]
            for c in range(len(spans)):
                own = next(o for o in range(ngrid) if moved(c, o) == m)
                if own % 2 and c == 1:
                    late.append(own)
                elif own % 2:
                    rs_copy(c, 0, own).start()
    for own in late:
        rs_copy(1, 0, own).start()

    def ag_copy(c, s, m):
        return remote(resid.at[at(c, m), :, spans[c]], resid.at[at(c, m), :, spans[c]], ag_s.at[c, m + (1 << s)], ag_r.at[c, m + (1 << s)], grid=at(c, 1 << s))

    def ag_wait(c, m):
        s = low_bit(m, bits)
        remote(resid.at[at(c, m), :, spans[c]], resid.at[at(c, m), :, spans[c]], ag_s.at[c, m], ag_r.at[c, m], grid=at(c, 1 << s)).wait_recv()

    def p_copy(c, m):
        piece = at(c, m)
        keeps = piece // per_row
        src, dst = resid.at[piece, :, spans[c]], prec.at[piece % per_row, r, :, spans[c]]
        return keeps, remote(src, dst, p_s.at[c, m], p_r.at[c, piece % per_row, r], row=keeps), pltpu.make_async_copy(src, dst, p_s.at[c, m])

    def pass_on(c, m):
        for s in reversed(range(low_bit(m, bits))):
            ag_copy(c, s, m).start()
        keeps, far, near = p_copy(c, m)

        @pl.when(keeps != r)
        def _():
            far.start()

        @pl.when(keeps == r)
        def _():
            near.start()

    ready = []

    def reduce(c, m):
        for s in range(low_bit(m, bits)):
            rs_copy(c, s, m | 1 << s).wait_recv()
            fit[at(c, m), :, spans[c], :] += rec[slots[s, m], :, spans[c], :]
        if m:
            rs_copy(c, low_bit(m, bits), m).start()
            return
        if not ready:
            ready.append(c)

            @pl.when(r != owner)
            def _():
                c_copy(1).wait_recv()
        resid[j, :, spans[c], :] = cbuf[:, spans[c], :] - fit[j, :, spans[c], :]
        pass_on(c, 0)

    def arrive(c, m):
        ag_wait(c, m)
        pass_on(c, m)

    def gradient(region, first):
        two = up[first:first + 2]
        span = regions[region]
        piece = jnp.concatenate([resid[at(0, m), i, span, :] for m in two for i in range(npp)], axis=1)
        t = [jnp.concatenate([buf[at(0, m)] for m in two], axis=0) for buf in (thi, tlo)]
        out = dot3(split(piece), t, ((1,), (0,)))
        outer[span, :] = out if first == 0 else outer[span, :] + out
        w = dot3(split(jnp.transpose(piece)), (xhi[span, :], xlo[span, :]), ((1,), (0,)))
        more = None
        for n, m in enumerate(two):
            for i in range(npp):
                p = at(0, m) * npp + i
                wp = w[n * width + i * vec:n * width + (i + 1) * vec, :]
                one = x8[pl.ds(p, 1), :] * wp
                more = one if more is None else more + one
                row = jnp.sum(wp * core_t[...], axis=0, keepdims=True)
                inner[pl.ds(p, 1), :] = row if region == 0 else inner[pl.ds(p, 1), :] + row
        cg_t[...] = more if region == 0 and first == 0 else cg_t[...] + more

    evens = [m for m in down if m % 2 == 0]
    lots = (evens, [m for m in up if m and m % 2 == 0], [m for m in up if m % 2])
    expected = (((8.8, 14.7), (18.0, 21.3), (20.0, 24.6)), ((14.0, 20.0), (23.3, 26.6), (25.5, 30.0)), ((9.5, 15.0), (17.5, 21.0), (21.1, 23.0)))
    when, events = {}, []
    for c in range(len(spans)):
        for kind, (lot, (begin, end)) in enumerate(zip(lots, expected[c])):
            for n, m in enumerate(lot):
                time = begin + (end - begin) * n / max(len(lot) - 1, 1)
                when[c, kind > 0, moved(c, m)] = time
                events.append((time, len(events), functools.partial(arrive if kind else reduce, c, m)))
    for region, parts in enumerate(((0,), (1, 2))):
        for first in range(0, ngrid, 2):
            time = (22.2, 26.8)[region] + (6.0, 2.0)[region] * first / ngrid
            time = max([time] + [when[c, m > 0, m] for c in parts for m in up[first:first + 2]])
            events.append((time, len(events), functools.partial(gradient, region, first)))

    core_t[...] = jnp.transpose(core_ref[...])
    for p in range(np_all):
        hi, lo = split(x8[p:p + 1, :] * core_t[...])
        thi[p // npp, p % npp * vec:(p % npp + 1) * vec, :] = hi
        tlo[p // npp, p % npp * vec:(p % npp + 1) * vec, :] = lo
    for _, _, event in sorted(events, key=lambda item: item[:2]):
        event()

    odd = r % 2
    mate = r + 1 - 2 * odd
    cg[...] = jnp.transpose(cg_t[...])
    k_copy = remote(cg.at[pl.ds((1 - odd) * half, half)], cg_core, k_s.at[0], k_r.at[0], row=mate)
    k_copy.start()

    def i_copy():
        return remote(inner, inner_rec.at[r - 1], i_s.at[0], i_r.at[r - 1], row=0)

    @pl.when(r != 0)
    def _():
        i_copy().start()

    k_copy.wait_recv()
    cg_half[...] = cg[pl.ds(odd * half, half), :] + cg_core[...]

    def h_copy(t):
        return remote(cg_half, cg_row.at[t - 1], h_s.at[t - 1], h_r.at[t - 1], row=(r + 2 * t) % nrow)

    for t in range(1, nrow // 2):
        h_copy(t).start()

    fg_ref[...] = fg_scale * outer[0:rows, :]

    @pl.when(r == 0)
    def _():
        acc = outer[0:np_all, :] + inner[...]
        for e in range(1, nrow):
            remote(inner, inner_rec.at[e - 1], i_s.at[0], i_r.at[e - 1], row=e).wait_recv()
            acc = acc + inner_rec[e - 1]
        fg_ref[0:np_all, :] = fg_scale * acc

    fg_out = pltpu.make_async_copy(fg_ref, fg_hbm, out_s.at[1])
    fg_out.start()

    for c in range(len(spans)):
        for m in range(ngrid):
            keeps, far, near = p_copy(c, m)

            @pl.when(keeps != r)
            def _():
                far.wait_send()

            @pl.when(keeps == r)
            def _():
                near.wait()
    for src in range(nrow):
        @pl.when(r != src)
        def _():
            for t in range(per_row):
                for c, span in enumerate(spans):
                    here = prec.at[t, src, :, span]
                    remote(here, here, p_s.at[0, 0], p_r.at[c, t, src], row=src).wait_recv()

        for t in range(per_row):
            for i in range(npp):
                res_ref[pl.ds(src * rows * held + t * npp + i, rows, stride=held), :] = prec[t, src, i, 0:rows, :]

    res_out = pltpu.make_async_copy(res_ref, res_hbm, out_s.at[0])
    res_out.start()

    acc = cg_half[...]
    for t in range(1, nrow // 2):
        h_copy(t).wait_recv()
        acc = acc + cg_row[t - 1]
    cg_fin[odd] = cg_scale * acc
    f_copy = remote(cg_fin.at[odd], cg_fin.at[odd], f_s.at[0], f_r.at[0], row=mate)
    f_copy.start()
    cg_ref[pl.ds(odd * half, half), :] = cg_fin[odd]
    f_copy.wait_recv()
    cg_ref[pl.ds((1 - odd) * half, half), :] = cg_fin[1 - odd]
    cg_out = pltpu.make_async_copy(cg_ref, cg_hbm, out_s.at[2])
    cg_out.start()

    @pl.when(r == 0)
    def _():
        for e in range(1, nrow):
            x8_copy(e).wait_send()

    @pl.when(r == owner)
    def _():
        for e in range(1, nrow):
            c_copy(e).wait_send()

    @pl.when(r != 0)
    def _():
        i_copy().wait_send()

    for c in range(len(spans)):
        for s in range(bits):
            for m in range(0, ngrid, 2 << s):
                rs_copy(c, s, m | 1 << s).wait_send()
                ag_copy(c, s, m).wait_send()
    for t in range(1, nrow // 2):
        h_copy(t).wait_send()
    k_copy.wait_send()
    f_copy.wait_send()
    res_out.wait()
    fg_out.wait()
    cg_out.wait()


def hand_out(res_in, cg_in, fg_in, res_out, cg_out, fg_out, res, cg, fg, sems):
    size = res_in.shape[0] // 4
    ways = [(fg_in, fg, fg_out), (cg_in, cg, cg_out)]
    for n in range(4):
        part = pl.ds(n * size, size)
        ways.append((res_in.at[part], res.at[part], res_out.at[part]))
    into = [pltpu.make_async_copy(src, mid, sems.at[0, n]) for n, (src, mid, _) in enumerate(ways)]
    out = [pltpu.make_async_copy(mid, dst, sems.at[1, n]) for n, (_, mid, dst) in enumerate(ways)]
    for copy in into:
        copy.start()
    for first, second in zip(into, out):
        first.wait()
        second.start()
    for copy in out:
        copy.wait()


def per_device(nrow, ngrid, cholesky, factor, core):
    held = cholesky.shape[0]
    rows, pts = factor.shape
    vec = core.shape[1]
    np_all = held * nrow
    npp = np_all // ngrid
    per_row = held // npp
    bits = ngrid.bit_length() - 1
    rpad = -(-rows // 16) * 16
    tiles = rpad // 16
    third = max(1, tiles // 6)
    sizes = [-(-(tiles - third) // 2) * 16, (tiles - third) // 2 * 16, third * 16]
    chunks = [(sum(sizes[:n]), size) for n, size in enumerate(sizes)]
    plain = list(range(bits))
    orders = [plain, plain, plain[1:] + plain[:1]]
    cg_scale = -1.0 / math.sqrt(np_all * rows * nrow)
    fg_scale = -math.sqrt(pts * ngrid / (rows * nrow * vec))
    cfg = (nrow, bits, npp, held, rows, rpad, vec, chunks, orders, cg_scale, fg_scale)

    slab = jnp.swapaxes(cholesky.reshape(held, nrow * rows, vec), 0, 1).reshape(nrow * rows * held, vec)

    piece = (npp, rpad, vec)
    nc = len(chunks)
    dma = pltpu.SemaphoreType.DMA
    hbm = pl.BlockSpec(memory_space=pltpu.HBM)
    f32 = lambda *shape: pltpu.VMEM(shape, F32)
    b16 = lambda *shape: pltpu.VMEM(shape, BF16)
    pairs = max(nrow // 2 - 1, 1)
    scratch = [
        f32(rows, pts), f32(rpad, pts), f32(pts, vec), f32(nrow * rows * held, vec), b16(rpad, pts), b16(rpad, pts),
        f32(np_all, pts), f32(np_all, pts, vec),
        b16(ngrid, pts, npp * vec), b16(ngrid, pts, npp * vec),
        f32(vec, pts), b16(ngrid, npp * vec, pts), b16(ngrid, npp * vec, pts),
        f32(ngrid, *piece), f32(ngrid - 1, *piece), f32(nrow, *piece), f32(*piece),
        f32(ngrid, *piece), f32(per_row, nrow, *piece),
        f32(rpad, pts), f32(vec, pts), f32(pts, vec),
        f32(nrow * rows * held, vec), f32(pts, vec), f32(rows, pts),
        f32(pts // 2, vec), f32(pts // 2, vec), f32(pairs, pts // 2, vec), f32(2, pts // 2, vec),
        f32(np_all, pts), f32(nrow - 1, np_all, pts),
        dma((3,)), dma((3,)), dma((nrow - 1,)), dma((1,)), dma((nrow - 1,)), dma((1,)),
        dma((nc, ngrid - 1)), dma((nc, ngrid - 1)), dma((nc, ngrid)), dma((nc, ngrid)),
        dma((nc, ngrid)), dma((nc, per_row, nrow)), dma((1,)), dma((nrow - 1,)),
        dma((1,)), dma((1,)), dma((pairs,)), dma((pairs,)), dma((1,)), dma((1,)),
    ]
    macs = 3 * rows * pts * np_all * vec
    results = (
        jax.ShapeDtypeStruct((nrow * rows * held, vec), F32),
        jax.ShapeDtypeStruct((pts, vec), F32),
        jax.ShapeDtypeStruct((rows, pts), F32),
    )
    made = pl.pallas_call(
        functools.partial(kernel, cfg),
        out_shape=results,
        in_specs=[hbm] * 3,
        out_specs=(hbm, hbm, hbm),
        scratch_shapes=scratch,
        cost_estimate=pl.CostEstimate(flops=6 * macs, bytes_accessed=8 * rows * pts, transcendentals=0),
        compiler_params=pltpu.CompilerParams(collective_id=0, has_side_effects=True, vmem_limit_bytes=62 * 2**20),
        name="hypercontraction",
    )(factor, core, slab)
    res, cg, fg = pl.pallas_call(
        hand_out,
        out_shape=results,
        in_specs=[pl.BlockSpec(memory_space=pl.ANY)] * 3,
        out_specs=(hbm, hbm, hbm),
        scratch_shapes=[f32(nrow * rows * held, vec), f32(pts, vec), f32(rows, pts), dma((2, 6))],
        name="hand_out",
    )(*made)
    res = jnp.swapaxes(res.reshape(nrow * rows, held, vec), 0, 1).reshape(held, nrow * rows * vec)
    return res, cg, fg


def solution(mesh):
    placed = (P("row", None), P("row", "grid"), P("grid", None))
    return jax.shard_map(
        functools.partial(per_device, mesh.shape["row"], mesh.shape["grid"]),
        mesh=mesh,
        in_specs=placed,
        out_specs=(P("row", None), P("grid", None), P("row", "grid")),
        check_vma=False,
    )
```

```python
import functools
import math

import jax
import jax.numpy as jnp
from jax import lax
from jax.experimental import pallas as pl
from jax.experimental.pallas import tpu as pltpu
from jax.sharding import PartitionSpec as P

MESH = pl.DeviceIdType.MESH
F32 = jnp.float32
BF16 = jnp.bfloat16


def split(x):
    hi = x.astype(BF16)
    return hi, (x - hi.astype(F32)).astype(BF16)


def dot3(left, right, dims):
    one = functools.partial(lax.dot_general, dimension_numbers=(dims, ((), ())), preferred_element_type=F32)
    return one(left[0], right[0]) + (one(left[0], right[1]) + one(left[1], right[0]))


def low_bit(m, bits):
    return next((s for s in range(bits) if m >> s & 1), bits)


def mirrored(m, bits):
    return sum((m >> s & 1) << (bits - 1 - s) for s in range(bits))


def kernel(cfg, x_hbm, core_hbm, chol_hbm, res_hbm, cg_hbm, fg_hbm,
           xraw, xpad, core_ref, chol, xhi, xlo, x8, x8b, vhi, vlo, core_t, thi, tlo, fit, rec, csend, cbuf, resid, prec, outer, cg_t, cg,
           res_ref, fg_ref,
           cg_core, cg_half, cg_row, cg_fin, inner, inner_rec,
           in_s, out_s, x8_s, x8_r, c_s, c_r, rs_s, rs_r, ag_s, ag_r, p_s, p_r, i_s, i_r, k_s, k_r, h_s, h_r, f_s, f_r):
    nrow, bits, npp, held, rows, rpad, vec, chunks, orders, cg_scale, fg_scale = cfg
    ngrid = 1 << bits
    np_all = npp * ngrid
    per_row = held // npp
    pts = x_hbm.shape[1]
    half = pts // 2
    r = lax.axis_index("row")
    j = lax.axis_index("grid")
    flips = [(1 - 2 * ((j // (1 << s)) % 2)) * (1 << s) for s in range(bits)]
    owner = j // per_row
    spans = [pl.ds(begin, size) for begin, size in chunks]
    regions = [pl.ds(0, chunks[1][0]), spans[1]]

    def moved(c, m):
        return sum(1 << orders[c][s] for s in range(bits) if m >> s & 1)

    def at(c, m):
        return j + sum(flips[s] for s in range(bits) if moved(c, m) >> s & 1)

    def remote(src, dst, ssem, rsem, **device):
        return pltpu.make_async_remote_copy(src_ref=src, dst_ref=dst, send_sem=ssem, recv_sem=rsem, device_id=device, device_id_type=MESH)

    x_in = pltpu.make_async_copy(x_hbm, xraw, in_s.at[0])
    core_in = pltpu.make_async_copy(core_hbm, core_ref, in_s.at[1])
    chol_in = pltpu.make_async_copy(chol_hbm, chol, in_s.at[2])
    x8_in = pltpu.make_async_copy(x_hbm.at[pl.ds(0, np_all)], x8, in_s.at[3])

    @pl.when(r == 0)
    def _():
        x8_in.start()

    x_in.start()
    core_in.start()
    chol_in.start()

    barrier = pltpu.get_barrier_semaphore()
    for e in range(1, nrow):
        pl.semaphore_signal(barrier, inc=1, device_id={"row": (r + e) % nrow}, device_id_type=MESH)
    for s in range(bits):
        pl.semaphore_signal(barrier, inc=1, device_id={"grid": at(0, 1 << s)}, device_id_type=MESH)
    pl.semaphore_wait(barrier, nrow - 1 + bits)

    def x8_copy(e):
        return remote(x8, x8, x8_s.at[e - 1], x8_r.at[0], row=(r + e) % nrow)

    def c_copy(e):
        to = (r + e) % nrow
        return remote(csend.at[to], cbuf, c_s.at[e - 1], c_r.at[0], row=to)

    @pl.when(r == 0)
    def _():
        x8_in.wait()
        for e in range(1, nrow):
            x8_copy(e).start()

    x_in.wait()
    if rpad > rows:
        xpad[rows:rpad, :] = jnp.zeros((rpad - rows, pts), F32)
    xpad[0:rows, :] = xraw[...]
    hi, lo = split(xpad[...])
    xhi[...] = hi
    xlo[...] = lo
    core_in.wait()

    @pl.when(r != 0)
    def _():
        x8_copy(1).wait_recv()

    flip = jnp.transpose(jnp.concatenate([x8[...], jnp.zeros((vec - np_all, pts), F32)], axis=0))
    for p in range(np_all):
        x8b[p] = jnp.broadcast_to(flip[:, p:p + 1], (pts, vec))

    slots = {}
    for s in range(bits):
        for m in range(0, ngrid, 2 << s):
            slots[s, m] = len(slots)

    def rs_copy(c, s, m):
        slot = slots[s, m ^ 1 << s]
        return remote(fit.at[at(c, m), :, spans[c]], rec.at[slot, :, spans[c]], rs_s.at[c, slot], rs_r.at[c, slot], grid=at(c, 1 << s))

    down = sorted(range(ngrid), key=lambda m: -mirrored(m, bits))
    up = down[::-1]
    width = npp * vec
    late = []

    def give_cholesky():
        chol_in.wait()
        for t in range(per_row):
            @pl.when((r == owner) & (j % per_row == t))
            def _():
                for to in range(nrow):
                    for i in range(npp):
                        if rpad > rows:
                            csend[to, i, rows:rpad, :] = jnp.zeros((rpad - rows, vec), F32)
                        csend[to, i, 0:rows, :] = chol[pl.ds(to * rows * held + t * npp + i, rows, stride=held), :]

        @pl.when(r == owner)
        def _():
            for e in range(1, nrow):
                c_copy(e).start()
            cbuf[...] = csend[r]

    for first in range(0, ngrid, 2):
        two = down[first:first + 2]
        for m in two:
            for i in range(npp):
                hi, lo = split(x8b[at(0, m) * npp + i] * core_ref[...])
                vhi[at(0, m), :, i * vec:(i + 1) * vec] = hi
                vlo[at(0, m), :, i * vec:(i + 1) * vec] = lo
        v = [jnp.concatenate([buf[at(0, m)] for m in two], axis=1) for buf in (vhi, vlo)]
        part = dot3((xhi[...], xlo[...]), v, ((1,), (0,)))
        for n, m in enumerate(two):
            for i in range(npp):
                fit[at(0, m), i] = part[:, n * width + i * vec:n * width + (i + 1) * vec]
            for c in range(len(spans)):
                own = next(o for o in range(ngrid) if moved(c, o) == m)
                if own % 2 and c == 1:
                    late.append(own)
                elif own % 2:
                    rs_copy(c, 0, own).start()
        if first == 0:
            give_cholesky()
    for own in late:
        rs_copy(1, 0, own).start()

    def ag_copy(c, s, m):
        return remote(resid.at[at(c, m), :, spans[c]], resid.at[at(c, m), :, spans[c]], ag_s.at[c, m + (1 << s)], ag_r.at[c, m + (1 << s)], grid=at(c, 1 << s))

    def ag_wait(c, m):
        s = low_bit(m, bits)
        remote(resid.at[at(c, m), :, spans[c]], resid.at[at(c, m), :, spans[c]], ag_s.at[c, m], ag_r.at[c, m], grid=at(c, 1 << s)).wait_recv()

    def p_copy(c, m):
        piece = at(c, m)
        keeps = piece // per_row
        src, dst = resid.at[piece, :, spans[c]], prec.at[piece % per_row, r, :, spans[c]]
        return keeps, remote(src, dst, p_s.at[c, m], p_r.at[c, piece % per_row, r], row=keeps), pltpu.make_async_copy(src, dst, p_s.at[c, m])

    def pass_on(c, m):
        for s in reversed(range(low_bit(m, bits))):
            ag_copy(c, s, m).start()
        keeps, far, near = p_copy(c, m)

        @pl.when(keeps != r)
        def _():
            far.start()

        @pl.when(keeps == r)
        def _():
            near.start()

    ready = []

    def reduce(c, m):
        for s in range(low_bit(m, bits)):
            rs_copy(c, s, m | 1 << s).wait_recv()
            fit[at(c, m), :, spans[c], :] += rec[slots[s, m], :, spans[c], :]
        if m:
            rs_copy(c, low_bit(m, bits), m).start()
            return
        if not ready:
            ready.append(c)

            @pl.when(r != owner)
            def _():
                c_copy(1).wait_recv()
        resid[j, :, spans[c], :] = cbuf[:, spans[c], :] - fit[j, :, spans[c], :]
        pass_on(c, 0)

    def arrive(c, m):
        ag_wait(c, m)
        pass_on(c, m)

    def gradient(region, first):
        two = up[first:first + 2]
        span = regions[region]
        piece = jnp.concatenate([resid[at(0, m), i, span, :] for m in two for i in range(npp)], axis=1)
        t = [jnp.concatenate([buf[at(0, m)] for m in two], axis=0) for buf in (thi, tlo)]
        out = dot3(split(piece), t, ((1,), (0,)))
        outer[span, :] = out if first == 0 else outer[span, :] + out
        w = dot3(split(jnp.transpose(piece)), (xhi[span, :], xlo[span, :]), ((1,), (0,)))
        more = None
        for n, m in enumerate(two):
            for i in range(npp):
                p = at(0, m) * npp + i
                wp = w[n * width + i * vec:n * width + (i + 1) * vec, :]
                one = x8[pl.ds(p, 1), :] * wp
                more = one if more is None else more + one
                row = jnp.sum(wp * core_t[...], axis=0, keepdims=True)
                inner[pl.ds(p, 1), :] = row if region == 0 else inner[pl.ds(p, 1), :] + row
        cg_t[...] = more if region == 0 and first == 0 else cg_t[...] + more

    evens = [m for m in down if m % 2 == 0]
    lots = (evens, [m for m in up if m and m % 2 == 0], [m for m in up if m % 2])
    expected = (((8.8, 14.7), (18.0, 21.3), (20.0, 24.6)), ((14.0, 20.0), (23.3, 26.6), (25.5, 30.0)), ((9.5, 15.0), (17.5, 21.0), (21.1, 23.0)))
    when, events = {}, []
    for c in range(len(spans)):
        for kind, (lot, (begin, end)) in enumerate(zip(lots, expected[c])):
            for n, m in enumerate(lot):
                time = begin + (end - begin) * n / max(len(lot) - 1, 1)
                when[c, kind > 0, moved(c, m)] = time
                events.append((time, len(events), functools.partial(arrive if kind else reduce, c, m)))
    for region, parts in enumerate(((0, 2), (1,))):
        for first in range(0, ngrid, 2):
            time = (22.2, 26.8)[region] + (6.0, 2.0)[region] * first / ngrid
            time = max([time] + [when[c, m > 0, m] for c in parts for m in up[first:first + 2]])
            events.append((time, len(events), functools.partial(gradient, region, first)))

    core_t[...] = jnp.transpose(core_ref[...])
    for p in range(np_all):
        hi, lo = split(x8[p:p + 1, :] * core_t[...])
        thi[p // npp, p % npp * vec:(p % npp + 1) * vec, :] = hi
        tlo[p // npp, p % npp * vec:(p % npp + 1) * vec, :] = lo
    for _, _, event in sorted(events, key=lambda item: item[:2]):
        event()

    odd = r % 2
    mate = r + 1 - 2 * odd
    mine = pl.multiple_of(odd * half, half)
    other = pl.multiple_of((1 - odd) * half, half)
    if half % 128:
        cg[...] = jnp.transpose(cg_t[...])
    else:
        cg[pl.ds(other, half), :] = jnp.transpose(cg_t[:, pl.ds(other, half)])
    k_copy = remote(cg.at[pl.ds(other, half)], cg_core, k_s.at[0], k_r.at[0], row=mate)
    k_copy.start()
    if half % 128 == 0:
        cg[pl.ds(mine, half), :] = jnp.transpose(cg_t[:, pl.ds(mine, half)])

    def i_copy():
        return remote(inner, inner_rec.at[r - 1], i_s.at[0], i_r.at[r - 1], row=0)

    @pl.when(r != 0)
    def _():
        i_copy().start()

    k_copy.wait_recv()
    cg_half[...] = cg[pl.ds(mine, half), :] + cg_core[...]
    block = half // 2

    def h_copy(n, t):
        part = pl.ds(n * block, block)
        return remote(cg_half.at[part], cg_row.at[t - 1, part], h_s.at[n, t - 1], h_r.at[n, t - 1], row=(r + 2 * t) % nrow)

    for n in range(2):
        for t in range(1, nrow // 2):
            h_copy(n, t).start()

    fg_ref[...] = fg_scale * outer[0:rows, :]

    @pl.when(r == 0)
    def _():
        acc = outer[0:np_all, :] + inner[...]
        for e in range(1, nrow):
            remote(inner, inner_rec.at[e - 1], i_s.at[0], i_r.at[e - 1], row=e).wait_recv()
            acc = acc + inner_rec[e - 1]
        fg_ref[0:np_all, :] = fg_scale * acc

    fg_out = pltpu.make_async_copy(fg_ref, fg_hbm, out_s.at[1])
    fg_out.start()

    for c in range(len(spans)):
        for m in range(ngrid):
            keeps, far, near = p_copy(c, m)

            @pl.when(keeps != r)
            def _():
                far.wait_send()

            @pl.when(keeps == r)
            def _():
                near.wait()
    for src in range(nrow):
        @pl.when(r != src)
        def _():
            for t in range(per_row):
                for c, span in enumerate(spans):
                    here = prec.at[t, src, :, span]
                    remote(here, here, p_s.at[0, 0], p_r.at[c, t, src], row=src).wait_recv()

        for t in range(per_row):
            for i in range(npp):
                res_ref[pl.ds(src * rows * held + t * npp + i, rows, stride=held), :] = prec[t, src, i, 0:rows, :]

    res_out = pltpu.make_async_copy(res_ref, res_hbm, out_s.at[0])
    res_out.start()

    def f_copy(n):
        dst = cg_hbm.at[pl.ds(pl.multiple_of(odd * half + n * block, block), block)]
        return remote(cg_fin.at[n], dst, f_s.at[n], f_r.at[n], row=mate), pltpu.make_async_copy(cg_fin.at[n], dst, out_s.at[2 + n])

    for n in range(2):
        part = pl.ds(n * block, block)
        acc = cg_half[part, :]
        for t in range(1, nrow // 2):
            h_copy(n, t).wait_recv()
            acc = acc + cg_row[t - 1, part, :]
        cg_fin[n] = cg_scale * acc
        for copy in f_copy(n):
            copy.start()
    for n in range(2):
        here = cg_hbm.at[pl.ds(pl.multiple_of((1 - odd) * half + n * block, block), block)]
        remote(cg_fin.at[n], here, f_s.at[n], f_r.at[n], row=mate).wait_recv()

    @pl.when(r == 0)
    def _():
        for e in range(1, nrow):
            x8_copy(e).wait_send()

    @pl.when(r == owner)
    def _():
        for e in range(1, nrow):
            c_copy(e).wait_send()

    @pl.when(r != 0)
    def _():
        i_copy().wait_send()

    for c in range(len(spans)):
        for s in range(bits):
            for m in range(0, ngrid, 2 << s):
                rs_copy(c, s, m | 1 << s).wait_send()
                ag_copy(c, s, m).wait_send()
    for n in range(2):
        for t in range(1, nrow // 2):
            h_copy(n, t).wait_send()
        far, near = f_copy(n)
        far.wait_send()
        near.wait()
    k_copy.wait_send()
    res_out.wait()
    fg_out.wait()


def hand_out(res_in, cg_in, fg_in, res_out, cg_out, fg_out, res, cg, fg, sems):
    ways = []
    for src, mid, dst, axis, parts in ((res_in, res, res_out, 0, 6), (fg_in, fg, fg_out, 1, 3), (cg_in, cg, cg_out, 0, 3)):
        size = src.shape[axis] // parts
        for n in range(parts):
            part = (slice(None),) * axis + (pl.ds(n * size, size),)
            ways.append((src.at[part], mid.at[part], dst.at[part]))
    into = [pltpu.make_async_copy(src, mid, sems.at[0, n]) for n, (src, mid, _) in enumerate(ways)]
    out = [pltpu.make_async_copy(mid, dst, sems.at[1, n]) for n, (_, mid, dst) in enumerate(ways)]
    for copy in into:
        copy.start()
    for first, second in zip(into, out):
        first.wait()
        second.start()
    for copy in out:
        copy.wait()


def per_device(nrow, ngrid, cholesky, factor, core):
    held = cholesky.shape[0]
    rows, pts = factor.shape
    vec = core.shape[1]
    np_all = held * nrow
    npp = np_all // ngrid
    per_row = held // npp
    bits = ngrid.bit_length() - 1
    rpad = -(-rows // 16) * 16
    tiles = rpad // 16
    third = max(1, tiles // 6)
    sizes = [-(-(tiles - third) // 2) * 16, (tiles - third) // 2 * 16, third * 16]
    chunks = [(0, sizes[0]), (sizes[0] + sizes[2], sizes[1]), (sizes[0], sizes[2])]
    plain = list(range(bits))
    orders = [plain, plain, plain[1:] + plain[:1]]
    cg_scale = -1.0 / math.sqrt(np_all * rows * nrow)
    fg_scale = -math.sqrt(pts * ngrid / (rows * nrow * vec))
    cfg = (nrow, bits, npp, held, rows, rpad, vec, chunks, orders, cg_scale, fg_scale)

    slab = jnp.swapaxes(cholesky.reshape(held, nrow * rows, vec), 0, 1).reshape(nrow * rows * held, vec)

    piece = (npp, rpad, vec)
    nc = len(chunks)
    dma = pltpu.SemaphoreType.DMA
    hbm = pl.BlockSpec(memory_space=pltpu.HBM)
    f32 = lambda *shape: pltpu.VMEM(shape, F32)
    b16 = lambda *shape: pltpu.VMEM(shape, BF16)
    pairs = max(nrow // 2 - 1, 1)
    scratch = [
        f32(rows, pts), f32(rpad, pts), f32(pts, vec), f32(nrow * rows * held, vec), b16(rpad, pts), b16(rpad, pts),
        f32(np_all, pts), f32(np_all, pts, vec),
        b16(ngrid, pts, npp * vec), b16(ngrid, pts, npp * vec),
        f32(vec, pts), b16(ngrid, npp * vec, pts), b16(ngrid, npp * vec, pts),
        f32(ngrid, *piece), f32(ngrid - 1, *piece), f32(nrow, *piece), f32(*piece),
        f32(ngrid, *piece), f32(per_row, nrow, *piece),
        f32(rpad, pts), f32(vec, pts), f32(pts, vec),
        f32(nrow * rows * held, vec), f32(rows, pts),
        f32(pts // 2, vec), f32(pts // 2, vec), f32(pairs, pts // 2, vec), f32(2, pts // 4, vec),
        f32(np_all, pts), f32(nrow - 1, np_all, pts),
        dma((4,)), dma((4,)), dma((nrow - 1,)), dma((1,)), dma((nrow - 1,)), dma((1,)),
        dma((nc, ngrid - 1)), dma((nc, ngrid - 1)), dma((nc, ngrid)), dma((nc, ngrid)),
        dma((nc, ngrid)), dma((nc, per_row, nrow)), dma((1,)), dma((nrow - 1,)),
        dma((1,)), dma((1,)), dma((2, pairs)), dma((2, pairs)), dma((2,)), dma((2,)),
    ]
    macs = 3 * rows * pts * np_all * vec
    results = (
        jax.ShapeDtypeStruct((nrow * rows * held, vec), F32),
        jax.ShapeDtypeStruct((pts, vec), F32),
        jax.ShapeDtypeStruct((rows, pts), F32),
    )
    made = pl.pallas_call(
        functools.partial(kernel, cfg),
        out_shape=results,
        in_specs=[hbm] * 3,
        out_specs=(hbm, hbm, hbm),
        scratch_shapes=scratch,
        cost_estimate=pl.CostEstimate(flops=6 * macs, bytes_accessed=8 * rows * pts, transcendentals=0),
        compiler_params=pltpu.CompilerParams(collective_id=0, has_side_effects=True, vmem_limit_bytes=62 * 2**20),
        name="hypercontraction",
    )(factor, core, slab)
    res, cg, fg = pl.pallas_call(
        hand_out,
        out_shape=results,
        in_specs=[pl.BlockSpec(memory_space=pl.ANY)] * 3,
        out_specs=(hbm, hbm, hbm),
        scratch_shapes=[f32(nrow * rows * held, vec), f32(pts, vec), f32(rows, pts), dma((2, 12))],
        name="hand_out",
    )(*made)
    res = jnp.swapaxes(res.reshape(nrow * rows, held, vec), 0, 1).reshape(held, nrow * rows * vec)
    return res, cg, fg


def solution(mesh):
    placed = (P("row", None), P("row", "grid"), P("grid", None))
    return jax.shard_map(
        functools.partial(per_device, mesh.shape["row"], mesh.shape["grid"]),
        mesh=mesh,
        in_specs=placed,
        out_specs=(P("row", None), P("grid", None), P("row", "grid")),
        check_vma=False,
    )
```

```python
import functools
import math

import jax
import jax.numpy as jnp
from jax import lax
from jax.experimental import pallas as pl
from jax.experimental.pallas import tpu as pltpu
from jax.sharding import PartitionSpec as P

MESH = pl.DeviceIdType.MESH
F32 = jnp.float32
BF16 = jnp.bfloat16


def split(x):
    hi = x.astype(BF16)
    return hi, (x - hi.astype(F32)).astype(BF16)


def dot3(left, right, dims):
    one = functools.partial(lax.dot_general, dimension_numbers=(dims, ((), ())), preferred_element_type=F32)
    return one(left[0], right[0]) + (one(left[0], right[1]) + one(left[1], right[0]))


def low_bit(m, bits):
    return next((s for s in range(bits) if m >> s & 1), bits)


def mirrored(m, bits):
    return sum((m >> s & 1) << (bits - 1 - s) for s in range(bits))


def kernel(cfg, x_hbm, core_hbm, chol_hbm, res_hbm, cg_hbm, fg_hbm,
           xraw, xpad, core_ref, chol, xhi, xlo, x8, x8b, vhi, vlo, core_t, thi, tlo, fit, rec, csend, cbuf, resid, prec, outer, cg_t, cg,
           res_ref, fg_ref,
           cg_core, cg_half, cg_row, cg_fin, inner, inner_rec,
           in_s, out_s, x8_s, x8_r, c_s, c_r, rs_s, rs_r, ag_s, ag_r, p_s, p_r, i_s, i_r, k_s, k_r, h_s, h_r, f_s, f_r):
    nrow, bits, npp, held, rows, rpad, vec, chunks, orders, cg_scale, fg_scale = cfg
    ngrid = 1 << bits
    np_all = npp * ngrid
    per_row = held // npp
    pts = x_hbm.shape[1]
    half = pts // 2
    r = lax.axis_index("row")
    j = lax.axis_index("grid")
    flips = [(1 - 2 * ((j // (1 << s)) % 2)) * (1 << s) for s in range(bits)]
    owner = j // per_row
    spans = [pl.ds(begin, size) for begin, size in chunks]
    regions = [pl.ds(0, chunks[1][0]), pl.ds(chunks[1][0], rpad - chunks[1][0])]

    def moved(c, m):
        return sum(1 << orders[c][s] for s in range(bits) if m >> s & 1)

    def at(c, m):
        return j + sum(flips[s] for s in range(bits) if moved(c, m) >> s & 1)

    def remote(src, dst, ssem, rsem, **device):
        return pltpu.make_async_remote_copy(src_ref=src, dst_ref=dst, send_sem=ssem, recv_sem=rsem, device_id=device, device_id_type=MESH)

    x_in = pltpu.make_async_copy(x_hbm, xraw, in_s.at[0])
    core_in = pltpu.make_async_copy(core_hbm, core_ref, in_s.at[1])
    chol_in = pltpu.make_async_copy(chol_hbm, chol, in_s.at[2])
    x8_in = pltpu.make_async_copy(x_hbm.at[pl.ds(0, np_all)], x8, in_s.at[3])

    @pl.when(r == 0)
    def _():
        x8_in.start()

    x_in.start()
    core_in.start()
    chol_in.start()

    barrier = pltpu.get_barrier_semaphore()
    for e in range(1, nrow):
        pl.semaphore_signal(barrier, inc=1, device_id={"row": (r + e) % nrow}, device_id_type=MESH)
    for s in range(bits):
        pl.semaphore_signal(barrier, inc=1, device_id={"grid": at(0, 1 << s)}, device_id_type=MESH)
    pl.semaphore_wait(barrier, nrow - 1 + bits)

    def x8_copy(e):
        return remote(x8, x8, x8_s.at[e - 1], x8_r.at[0], row=(r + e) % nrow)

    def c_copy(e):
        to = (r + e) % nrow
        return remote(csend.at[to], cbuf, c_s.at[e - 1], c_r.at[0], row=to)

    @pl.when(r == 0)
    def _():
        x8_in.wait()
        for e in range(1, nrow):
            x8_copy(e).start()

    x_in.wait()
    if rpad > rows:
        xpad[rows:rpad, :] = jnp.zeros((rpad - rows, pts), F32)
    xpad[0:rows, :] = xraw[...]
    hi, lo = split(xpad[...])
    xhi[...] = hi
    xlo[...] = lo
    core_in.wait()

    @pl.when(r != 0)
    def _():
        x8_copy(1).wait_recv()

    flip = jnp.transpose(jnp.concatenate([x8[...], jnp.zeros((vec - np_all, pts), F32)], axis=0))
    for p in range(np_all):
        x8b[p] = jnp.broadcast_to(flip[:, p:p + 1], (pts, vec))

    slots = {}
    for s in range(bits):
        for m in range(0, ngrid, 2 << s):
            slots[s, m] = len(slots)

    def rs_copy(c, s, m):
        slot = slots[s, m ^ 1 << s]
        return remote(fit.at[at(c, m), :, spans[c]], rec.at[slot, :, spans[c]], rs_s.at[c, slot], rs_r.at[c, slot], grid=at(c, 1 << s))

    down = sorted(range(ngrid), key=lambda m: -mirrored(m, bits))
    up = down[::-1]
    width = npp * vec
    late = {1: [], 3: []}

    def give_cholesky():
        chol_in.wait()
        for t in range(per_row):
            @pl.when((r == owner) & (j % per_row == t))
            def _():
                for to in range(nrow):
                    for i in range(npp):
                        if rpad > rows:
                            csend[to, i, rows:rpad, :] = jnp.zeros((rpad - rows, vec), F32)
                        csend[to, i, 0:rows, :] = chol[pl.ds(to * rows * held + t * npp + i, rows, stride=held), :]

        @pl.when(r == owner)
        def _():
            for e in range(1, nrow):
                c_copy(e).start()
            cbuf[...] = csend[r]

    for first in range(0, ngrid, 2):
        two = down[first:first + 2]
        for m in two:
            for i in range(npp):
                hi, lo = split(x8b[at(0, m) * npp + i] * core_ref[...])
                vhi[at(0, m), :, i * vec:(i + 1) * vec] = hi
                vlo[at(0, m), :, i * vec:(i + 1) * vec] = lo
        v = [jnp.concatenate([buf[at(0, m)] for m in two], axis=1) for buf in (vhi, vlo)]
        part = dot3((xhi[...], xlo[...]), v, ((1,), (0,)))
        for n, m in enumerate(two):
            for i in range(npp):
                fit[at(0, m), i] = part[:, n * width + i * vec:n * width + (i + 1) * vec]
            for c in range(len(spans)):
                own = next(o for o in range(ngrid) if moved(c, o) == m)
                if own % 2 and c in late:
                    late[c].append(own)
                elif own % 2:
                    rs_copy(c, 0, own).start()
        if first == 0:
            give_cholesky()
    for c, owns in late.items():
        for own in owns:
            rs_copy(c, 0, own).start()

    def ag_copy(c, s, m):
        return remote(resid.at[at(c, m), :, spans[c]], resid.at[at(c, m), :, spans[c]], ag_s.at[c, m + (1 << s)], ag_r.at[c, m + (1 << s)], grid=at(c, 1 << s))

    def ag_wait(c, m):
        s = low_bit(m, bits)
        remote(resid.at[at(c, m), :, spans[c]], resid.at[at(c, m), :, spans[c]], ag_s.at[c, m], ag_r.at[c, m], grid=at(c, 1 << s)).wait_recv()

    def p_copy(c, m):
        piece = at(c, m)
        keeps = piece // per_row
        src, dst = resid.at[piece, :, spans[c]], prec.at[piece % per_row, r, :, spans[c]]
        return keeps, remote(src, dst, p_s.at[c, m], p_r.at[c, piece % per_row, r], row=keeps), pltpu.make_async_copy(src, dst, p_s.at[c, m])

    def pass_on(c, m):
        for s in reversed(range(low_bit(m, bits))):
            ag_copy(c, s, m).start()
        keeps, far, near = p_copy(c, m)

        @pl.when(keeps != r)
        def _():
            far.start()

        @pl.when(keeps == r)
        def _():
            near.start()

    ready = []

    def reduce(c, m):
        for s in range(low_bit(m, bits)):
            rs_copy(c, s, m | 1 << s).wait_recv()
            fit[at(c, m), :, spans[c], :] += rec[slots[s, m], :, spans[c], :]
        if m:
            rs_copy(c, low_bit(m, bits), m).start()
            return
        if not ready:
            ready.append(c)

            @pl.when(r != owner)
            def _():
                c_copy(1).wait_recv()
        resid[j, :, spans[c], :] = cbuf[:, spans[c], :] - fit[j, :, spans[c], :]
        pass_on(c, 0)

    def arrive(c, m):
        ag_wait(c, m)
        pass_on(c, m)

    def gradient(region, first):
        two = up[first:first + 2]
        span = regions[region]
        piece = jnp.concatenate([resid[at(0, m), i, span, :] for m in two for i in range(npp)], axis=1)
        t = [jnp.concatenate([buf[at(0, m)] for m in two], axis=0) for buf in (thi, tlo)]
        out = dot3(split(piece), t, ((1,), (0,)))
        outer[span, :] = out if first == 0 else outer[span, :] + out
        w = dot3(split(jnp.transpose(piece)), (xhi[span, :], xlo[span, :]), ((1,), (0,)))
        more = None
        for n, m in enumerate(two):
            for i in range(npp):
                p = at(0, m) * npp + i
                wp = w[n * width + i * vec:n * width + (i + 1) * vec, :]
                one = x8[pl.ds(p, 1), :] * wp
                more = one if more is None else more + one
                row = jnp.sum(wp * core_t[...], axis=0, keepdims=True)
                inner[pl.ds(p, 1), :] = row if region == 0 else inner[pl.ds(p, 1), :] + row
        cg_t[...] = more if region == 0 and first == 0 else cg_t[...] + more

    evens = [m for m in down if m % 2 == 0]
    lots = (evens, [m for m in up if m and m % 2 == 0], [m for m in up if m % 2])
    expected = (
        ((8.4, 13.4), (16.4, 19.4), (17.0, 20.8)),
        ((12.4, 17.4), (20.4, 23.4), (21.0, 25.0)),
        ((9.5, 15.0), (17.5, 20.0), (20.1, 22.0)),
        ((16.0, 20.0), (22.7, 25.3), (24.0, 28.0)),
    )
    when, events = {}, []
    for c in range(len(spans)):
        for kind, (lot, (begin, end)) in enumerate(zip(lots, expected[c])):
            for n, m in enumerate(lot):
                time = begin + (end - begin) * n / max(len(lot) - 1, 1)
                when[c, kind > 0, moved(c, m)] = time
                events.append((time, len(events), functools.partial(arrive if kind else reduce, c, m)))
    for region, parts in enumerate(((0, 2), (1, 3))):
        for first in range(0, ngrid, 2):
            time = (20.5, 25.5)[region] + (5.0, 2.0)[region] * first / ngrid
            time = max([time] + [when[c, m > 0, m] for c in parts for m in up[first:first + 2]])
            events.append((time, len(events), functools.partial(gradient, region, first)))

    def turned_factors():
        core_t[...] = jnp.transpose(core_ref[...])
        for p in range(np_all):
            hi, lo = split(x8[p:p + 1, :] * core_t[...])
            thi[p // npp, p % npp * vec:(p % npp + 1) * vec, :] = hi
            tlo[p // npp, p % npp * vec:(p % npp + 1) * vec, :] = lo

    events.append((15.5, len(events), turned_factors))
    for _, _, event in sorted(events, key=lambda item: item[:2]):
        event()

    odd = r % 2
    mate = r + 1 - 2 * odd
    mine = pl.multiple_of(odd * half, half)
    other = pl.multiple_of((1 - odd) * half, half)
    if half % 128:
        cg[...] = jnp.transpose(cg_t[...])
    else:
        cg[pl.ds(other, half), :] = jnp.transpose(cg_t[:, pl.ds(other, half)])
    k_copy = remote(cg.at[pl.ds(other, half)], cg_core, k_s.at[0], k_r.at[0], row=mate)
    k_copy.start()
    if half % 128 == 0:
        cg[pl.ds(mine, half), :] = jnp.transpose(cg_t[:, pl.ds(mine, half)])

    def i_copy():
        return remote(inner, inner_rec.at[r - 1], i_s.at[0], i_r.at[r - 1], row=0)

    @pl.when(r != 0)
    def _():
        i_copy().start()

    k_copy.wait_recv()
    cg_half[...] = cg[pl.ds(mine, half), :] + cg_core[...]
    block = half // 2

    def h_copy(n, t):
        part = pl.ds(n * block, block)
        return remote(cg_half.at[part], cg_row.at[t - 1, part], h_s.at[n, t - 1], h_r.at[n, t - 1], row=(r + 2 * t) % nrow)

    for n in range(2):
        for t in range(1, nrow // 2):
            h_copy(n, t).start()

    fg_ref[...] = fg_scale * outer[0:rows, :]

    @pl.when(r == 0)
    def _():
        acc = outer[0:np_all, :] + inner[...]
        for e in range(1, nrow):
            remote(inner, inner_rec.at[e - 1], i_s.at[0], i_r.at[e - 1], row=e).wait_recv()
            acc = acc + inner_rec[e - 1]
        fg_ref[0:np_all, :] = fg_scale * acc

    fg_out = pltpu.make_async_copy(fg_ref, fg_hbm, out_s.at[1])
    fg_out.start()

    for c in range(len(spans)):
        for m in range(ngrid):
            keeps, far, near = p_copy(c, m)

            @pl.when(keeps != r)
            def _():
                far.wait_send()

            @pl.when(keeps == r)
            def _():
                near.wait()
    for src in range(nrow):
        @pl.when(r != src)
        def _():
            for t in range(per_row):
                for c, span in enumerate(spans):
                    here = prec.at[t, src, :, span]
                    remote(here, here, p_s.at[0, 0], p_r.at[c, t, src], row=src).wait_recv()

        for t in range(per_row):
            for i in range(npp):
                res_ref[pl.ds(src * rows * held + t * npp + i, rows, stride=held), :] = prec[t, src, i, 0:rows, :]

    res_out = pltpu.make_async_copy(res_ref, res_hbm, out_s.at[0])
    res_out.start()

    def f_copy(n):
        dst = cg_hbm.at[pl.ds(pl.multiple_of(odd * half + n * block, block), block)]
        return remote(cg_fin.at[n], dst, f_s.at[n], f_r.at[n], row=mate), pltpu.make_async_copy(cg_fin.at[n], dst, out_s.at[2 + n])

    for n in range(2):
        part = pl.ds(n * block, block)
        acc = cg_half[part, :]
        for t in range(1, nrow // 2):
            h_copy(n, t).wait_recv()
            acc = acc + cg_row[t - 1, part, :]
        cg_fin[n] = cg_scale * acc
        for copy in f_copy(n):
            copy.start()
    for n in range(2):
        here = cg_hbm.at[pl.ds(pl.multiple_of((1 - odd) * half + n * block, block), block)]
        remote(cg_fin.at[n], here, f_s.at[n], f_r.at[n], row=mate).wait_recv()

    @pl.when(r == 0)
    def _():
        for e in range(1, nrow):
            x8_copy(e).wait_send()

    @pl.when(r == owner)
    def _():
        for e in range(1, nrow):
            c_copy(e).wait_send()

    @pl.when(r != 0)
    def _():
        i_copy().wait_send()

    for c in range(len(spans)):
        for s in range(bits):
            for m in range(0, ngrid, 2 << s):
                rs_copy(c, s, m | 1 << s).wait_send()
                ag_copy(c, s, m).wait_send()
    for n in range(2):
        for t in range(1, nrow // 2):
            h_copy(n, t).wait_send()
        far, near = f_copy(n)
        far.wait_send()
        near.wait()
    k_copy.wait_send()
    res_out.wait()
    fg_out.wait()


def hand_out(res_in, cg_in, fg_in, res_out, cg_out, fg_out, res, cg, fg, sems):
    ways = []
    for src, mid, dst, axis, parts in ((res_in, res, res_out, 0, 6), (fg_in, fg, fg_out, 1, 3), (cg_in, cg, cg_out, 0, 3)):
        size = src.shape[axis] // parts
        for n in range(parts):
            part = (slice(None),) * axis + (pl.ds(n * size, size),)
            ways.append((src.at[part], mid.at[part], dst.at[part]))
    into = [pltpu.make_async_copy(src, mid, sems.at[0, n]) for n, (src, mid, _) in enumerate(ways)]
    out = [pltpu.make_async_copy(mid, dst, sems.at[1, n]) for n, (_, mid, dst) in enumerate(ways)]
    for copy in into:
        copy.start()
    for first, second in zip(into, out):
        first.wait()
        second.start()
    for copy in out:
        copy.wait()


def per_device(nrow, ngrid, cholesky, factor, core):
    held = cholesky.shape[0]
    rows, pts = factor.shape
    vec = core.shape[1]
    np_all = held * nrow
    npp = np_all // ngrid
    per_row = held // npp
    bits = ngrid.bit_length() - 1
    rpad = -(-rows // 16) * 16
    tiles = rpad // 16
    third = max(1, tiles // 6)
    fourth = (tiles - third) // 4
    rest = tiles - third - fourth
    sizes = [(rest - rest // 2) * 16, rest // 2 * 16, third * 16, fourth * 16]
    chunks = [(0, sizes[0]), (sizes[0] + sizes[2], sizes[1]), (sizes[0], sizes[2]), (rpad - sizes[3], sizes[3])]
    plain = list(range(bits))
    orders = [plain, plain, plain[1:] + plain[:1], plain]
    cg_scale = -1.0 / math.sqrt(np_all * rows * nrow)
    fg_scale = -math.sqrt(pts * ngrid / (rows * nrow * vec))
    cfg = (nrow, bits, npp, held, rows, rpad, vec, chunks, orders, cg_scale, fg_scale)

    slab = jnp.swapaxes(cholesky.reshape(held, nrow * rows, vec), 0, 1).reshape(nrow * rows * held, vec)

    piece = (npp, rpad, vec)
    nc = len(chunks)
    dma = pltpu.SemaphoreType.DMA
    hbm = pl.BlockSpec(memory_space=pltpu.HBM)
    f32 = lambda *shape: pltpu.VMEM(shape, F32)
    b16 = lambda *shape: pltpu.VMEM(shape, BF16)
    pairs = max(nrow // 2 - 1, 1)
    scratch = [
        f32(rows, pts), f32(rpad, pts), f32(pts, vec), f32(nrow * rows * held, vec), b16(rpad, pts), b16(rpad, pts),
        f32(np_all, pts), f32(np_all, pts, vec),
        b16(ngrid, pts, npp * vec), b16(ngrid, pts, npp * vec),
        f32(vec, pts), b16(ngrid, npp * vec, pts), b16(ngrid, npp * vec, pts),
        f32(ngrid, *piece), f32(ngrid - 1, *piece), f32(nrow, *piece), f32(*piece),
        f32(ngrid, *piece), f32(per_row, nrow, *piece),
        f32(rpad, pts), f32(vec, pts), f32(pts, vec),
        f32(nrow * rows * held, vec), f32(rows, pts),
        f32(pts // 2, vec), f32(pts // 2, vec), f32(pairs, pts // 2, vec), f32(2, pts // 4, vec),
        f32(np_all, pts), f32(nrow - 1, np_all, pts),
        dma((4,)), dma((4,)), dma((nrow - 1,)), dma((1,)), dma((nrow - 1,)), dma((1,)),
        dma((nc, ngrid - 1)), dma((nc, ngrid - 1)), dma((nc, ngrid)), dma((nc, ngrid)),
        dma((nc, ngrid)), dma((nc, per_row, nrow)), dma((1,)), dma((nrow - 1,)),
        dma((1,)), dma((1,)), dma((2, pairs)), dma((2, pairs)), dma((2,)), dma((2,)),
    ]
    macs = 3 * rows * pts * np_all * vec
    results = (
        jax.ShapeDtypeStruct((nrow * rows * held, vec), F32),
        jax.ShapeDtypeStruct((pts, vec), F32),
        jax.ShapeDtypeStruct((rows, pts), F32),
    )
    made = pl.pallas_call(
        functools.partial(kernel, cfg),
        out_shape=results,
        in_specs=[hbm] * 3,
        out_specs=(hbm, hbm, hbm),
        scratch_shapes=scratch,
        cost_estimate=pl.CostEstimate(flops=6 * macs, bytes_accessed=8 * rows * pts, transcendentals=0),
        compiler_params=pltpu.CompilerParams(collective_id=0, has_side_effects=True, vmem_limit_bytes=62 * 2**20),
        name="hypercontraction",
    )(factor, core, slab)
    res, cg, fg = pl.pallas_call(
        hand_out,
        out_shape=results,
        in_specs=[pl.BlockSpec(memory_space=pl.ANY)] * 3,
        out_specs=(hbm, hbm, hbm),
        scratch_shapes=[f32(nrow * rows * held, vec), f32(pts, vec), f32(rows, pts), dma((2, 12))],
        name="hand_out",
    )(*made)
    res = jnp.swapaxes(res.reshape(nrow * rows, held, vec), 0, 1).reshape(held, nrow * rows * vec)
    return res, cg, fg


def solution(mesh):
    placed = (P("row", None), P("row", "grid"), P("grid", None))
    return jax.shard_map(
        functools.partial(per_device, mesh.shape["row"], mesh.shape["grid"]),
        mesh=mesh,
        in_specs=placed,
        out_specs=(P("row", None), P("grid", None), P("row", "grid")),
        check_vma=False,
    )
```

```python
import functools
import math

import jax
import jax.numpy as jnp
from jax import lax
from jax.experimental import pallas as pl
from jax.experimental.pallas import tpu as pltpu
from jax.sharding import PartitionSpec as P

MESH = pl.DeviceIdType.MESH
F32 = jnp.float32
BF16 = jnp.bfloat16


def split(x):
    hi = x.astype(BF16)
    return hi, (x - hi.astype(F32)).astype(BF16)


def dot3(left, right, dims):
    one = functools.partial(lax.dot_general, dimension_numbers=(dims, ((), ())), preferred_element_type=F32)
    return one(left[0], right[0]) + (one(left[0], right[1]) + one(left[1], right[0]))


def low_bit(m, bits):
    return next((s for s in range(bits) if m >> s & 1), bits)


def mirrored(m, bits):
    return sum((m >> s & 1) << (bits - 1 - s) for s in range(bits))


def kernel(cfg, x_hbm, core_hbm, chol_hbm, res_hbm, cg_hbm, fg_hbm,
           xraw, xpad, core_ref, chol, xhi, xlo, x8, x8b, vhi, vlo, core_t, thi, tlo, fit, rec, csend, cbuf, resid, prec, outer, cg_t, cg,
           res_ref, fg_ref,
           cg_core, cg_half, cg_row, cg_fin, inner, inner_rec,
           in_s, out_s, x8_s, x8_r, c_s, c_r, rs_s, rs_r, ag_s, ag_r, p_s, p_r, i_s, i_r, k_s, k_r, h_s, h_r, f_s, f_r):
    nrow, bits, npp, held, rows, rpad, vec, chunks, orders, cg_scale, fg_scale = cfg
    ngrid = 1 << bits
    np_all = npp * ngrid
    per_row = held // npp
    pts = x_hbm.shape[1]
    half = pts // 2
    r = lax.axis_index("row")
    j = lax.axis_index("grid")
    flips = [(1 - 2 * ((j // (1 << s)) % 2)) * (1 << s) for s in range(bits)]
    owner = j // per_row
    spans = [pl.ds(begin, size) for begin, size in chunks]
    regions = [pl.ds(0, chunks[1][0]), spans[1]]

    def moved(c, m):
        return sum(1 << orders[c][s] for s in range(bits) if m >> s & 1)

    def at(c, m):
        return j + sum(flips[s] for s in range(bits) if moved(c, m) >> s & 1)

    def remote(src, dst, ssem, rsem, **device):
        return pltpu.make_async_remote_copy(src_ref=src, dst_ref=dst, send_sem=ssem, recv_sem=rsem, device_id=device, device_id_type=MESH)

    x_in = pltpu.make_async_copy(x_hbm, xraw, in_s.at[0])
    core_in = pltpu.make_async_copy(core_hbm, core_ref, in_s.at[1])
    chol_in = pltpu.make_async_copy(chol_hbm, chol, in_s.at[2])
    x8_in = pltpu.make_async_copy(x_hbm.at[pl.ds(0, np_all)], x8, in_s.at[3])

    @pl.when(r == 0)
    def _():
        x8_in.start()

    x_in.start()
    core_in.start()
    chol_in.start()

    barrier = pltpu.get_barrier_semaphore()
    for e in range(1, nrow):
        pl.semaphore_signal(barrier, inc=1, device_id={"row": (r + e) % nrow}, device_id_type=MESH)
    for s in range(bits):
        pl.semaphore_signal(barrier, inc=1, device_id={"grid": at(0, 1 << s)}, device_id_type=MESH)
    pl.semaphore_wait(barrier, nrow - 1 + bits)

    def x8_copy(e):
        return remote(x8, x8, x8_s.at[e - 1], x8_r.at[0], row=(r + e) % nrow)

    def c_copy(e):
        to = (r + e) % nrow
        return remote(csend.at[to], cbuf, c_s.at[e - 1], c_r.at[0], row=to)

    @pl.when(r == 0)
    def _():
        x8_in.wait()
        for e in range(1, nrow):
            x8_copy(e).start()

    x_in.wait()
    if rpad > rows:
        xpad[rows:rpad, :] = jnp.zeros((rpad - rows, pts), F32)
    xpad[0:rows, :] = xraw[...]
    hi, lo = split(xpad[...])
    xhi[...] = hi
    xlo[...] = lo
    core_in.wait()

    @pl.when(r != 0)
    def _():
        x8_copy(1).wait_recv()

    flip = jnp.transpose(jnp.concatenate([x8[...], jnp.zeros((vec - np_all, pts), F32)], axis=0))
    for p in range(np_all):
        x8b[p] = jnp.broadcast_to(flip[:, p:p + 1], (pts, vec))

    slots = {}
    for s in range(bits):
        for m in range(0, ngrid, 2 << s):
            slots[s, m] = len(slots)

    def rs_copy(c, s, m):
        slot = slots[s, m ^ 1 << s]
        return remote(fit.at[at(c, m), :, spans[c]], rec.at[slot, :, spans[c]], rs_s.at[c, slot], rs_r.at[c, slot], grid=at(c, 1 << s))

    down = sorted(range(ngrid), key=lambda m: -mirrored(m, bits))
    up = down[::-1]
    width = npp * vec
    late = []

    def give_cholesky():
        chol_in.wait()
        for t in range(per_row):
            @pl.when((r == owner) & (j % per_row == t))
            def _():
                for to in range(nrow):
                    for i in range(npp):
                        if rpad > rows:
                            csend[to, i, rows:rpad, :] = jnp.zeros((rpad - rows, vec), F32)
                        csend[to, i, 0:rows, :] = chol[pl.ds(to * rows * held + t * npp + i, rows, stride=held), :]

        @pl.when(r == owner)
        def _():
            for e in range(1, nrow):
                c_copy(e).start()
            cbuf[...] = csend[r]

    for first in range(0, ngrid, 2):
        two = down[first:first + 2]
        for m in two:
            for i in range(npp):
                hi, lo = split(x8b[at(0, m) * npp + i] * core_ref[...])
                vhi[at(0, m), :, i * vec:(i + 1) * vec] = hi
                vlo[at(0, m), :, i * vec:(i + 1) * vec] = lo
        v = [jnp.concatenate([buf[at(0, m)] for m in two], axis=1) for buf in (vhi, vlo)]
        part = dot3((xhi[...], xlo[...]), v, ((1,), (0,)))
        for n, m in enumerate(two):
            for i in range(npp):
                fit[at(0, m), i] = part[:, n * width + i * vec:n * width + (i + 1) * vec]
            for c in range(len(spans)):
                own = next(o for o in range(ngrid) if moved(c, o) == m)
                if own % 2 and c == 1:
                    late.append(own)
                elif own % 2:
                    rs_copy(c, 0, own).start()
        if first == 0:
            give_cholesky()
    for own in late:
        rs_copy(1, 0, own).start()

    def ag_copy(c, s, m):
        return remote(resid.at[at(c, m), :, spans[c]], resid.at[at(c, m), :, spans[c]], ag_s.at[c, m + (1 << s)], ag_r.at[c, m + (1 << s)], grid=at(c, 1 << s))

    def ag_wait(c, m):
        s = low_bit(m, bits)
        remote(resid.at[at(c, m), :, spans[c]], resid.at[at(c, m), :, spans[c]], ag_s.at[c, m], ag_r.at[c, m], grid=at(c, 1 << s)).wait_recv()

    def p_copy(c, m):
        piece = at(c, m)
        keeps = piece // per_row
        src, dst = resid.at[piece, :, spans[c]], prec.at[piece % per_row, r, :, spans[c]]
        return keeps, remote(src, dst, p_s.at[c, m], p_r.at[c, piece % per_row, r], row=keeps), pltpu.make_async_copy(src, dst, p_s.at[c, m])

    def pass_on(c, m):
        for s in reversed(range(low_bit(m, bits))):
            ag_copy(c, s, m).start()
        keeps, far, near = p_copy(c, m)

        @pl.when(keeps != r)
        def _():
            far.start()

        @pl.when(keeps == r)
        def _():
            near.start()

    ready = []

    def reduce(c, m):
        for s in range(low_bit(m, bits)):
            rs_copy(c, s, m | 1 << s).wait_recv()
            fit[at(c, m), :, spans[c], :] += rec[slots[s, m], :, spans[c], :]
        if m:
            rs_copy(c, low_bit(m, bits), m).start()
            return
        if not ready:
            ready.append(c)

            @pl.when(r != owner)
            def _():
                c_copy(1).wait_recv()
        resid[j, :, spans[c], :] = cbuf[:, spans[c], :] - fit[j, :, spans[c], :]
        pass_on(c, 0)

    def arrive(c, m):
        ag_wait(c, m)
        pass_on(c, m)

    def gradient(region, first):
        two = up[first:first + 2]
        span = regions[region]
        piece = jnp.concatenate([resid[at(0, m), i, span, :] for m in two for i in range(npp)], axis=1)
        t = [jnp.concatenate([buf[at(0, m)] for m in two], axis=0) for buf in (thi, tlo)]
        out = dot3(split(piece), t, ((1,), (0,)))
        outer[span, :] = out if first == 0 else outer[span, :] + out
        w = dot3(split(jnp.transpose(piece)), (xhi[span, :], xlo[span, :]), ((1,), (0,)))
        more = None
        for n, m in enumerate(two):
            for i in range(npp):
                p = at(0, m) * npp + i
                wp = w[n * width + i * vec:n * width + (i + 1) * vec, :]
                one = x8[pl.ds(p, 1), :] * wp
                more = one if more is None else more + one
                row = jnp.sum(wp * core_t[...], axis=0, keepdims=True)
                inner[pl.ds(p, 1), :] = row if region == 0 else inner[pl.ds(p, 1), :] + row
        cg_t[...] = more if region == 0 and first == 0 else cg_t[...] + more

    evens = [m for m in down if m % 2 == 0]
    lots = (evens, [m for m in up if m and m % 2 == 0], [m for m in up if m % 2])
    expected = (((8.8, 14.7), (18.0, 21.3), (20.0, 24.6)), ((14.0, 20.0), (23.3, 26.6), (25.5, 30.0)), ((9.5, 15.0), (17.5, 21.0), (21.1, 23.0)))
    when, events = {}, []
    for c in range(len(spans)):
        for kind, (lot, (begin, end)) in enumerate(zip(lots, expected[c])):
            for n, m in enumerate(lot):
                time = begin + (end - begin) * n / max(len(lot) - 1, 1)
                when[c, kind > 0, moved(c, m)] = time
                events.append((time, len(events), functools.partial(arrive if kind else reduce, c, m)))
    for region, parts in enumerate(((0, 2), (1,))):
        for first in range(0, ngrid, 2):
            time = (22.2, 26.8)[region] + (6.0, 2.0)[region] * first / ngrid
            time = max([time] + [when[c, m > 0, m] for c in parts for m in up[first:first + 2]])
            events.append((time, len(events), functools.partial(gradient, region, first)))

    def turned_factors():
        core_t[...] = jnp.transpose(core_ref[...])
        for p in range(np_all):
            hi, lo = split(x8[p:p + 1, :] * core_t[...])
            thi[p // npp, p % npp * vec:(p % npp + 1) * vec, :] = hi
            tlo[p // npp, p % npp * vec:(p % npp + 1) * vec, :] = lo

    events.append((16.5, len(events), turned_factors))
    for _, _, event in sorted(events, key=lambda item: item[:2]):
        event()

    odd = r % 2
    mate = r + 1 - 2 * odd
    mine = pl.multiple_of(odd * half, half)
    other = pl.multiple_of((1 - odd) * half, half)
    if half % 128:
        cg[...] = jnp.transpose(cg_t[...])
    else:
        cg[pl.ds(other, half), :] = jnp.transpose(cg_t[:, pl.ds(other, half)])
    k_copy = remote(cg.at[pl.ds(other, half)], cg_core, k_s.at[0], k_r.at[0], row=mate)
    k_copy.start()
    if half % 128 == 0:
        cg[pl.ds(mine, half), :] = jnp.transpose(cg_t[:, pl.ds(mine, half)])

    def i_copy():
        return remote(inner, inner_rec.at[r - 1], i_s.at[0], i_r.at[r - 1], row=0)

    @pl.when(r != 0)
    def _():
        i_copy().start()

    k_copy.wait_recv()
    cg_half[...] = cg[pl.ds(mine, half), :] + cg_core[...]
    block = half // 2

    def h_copy(n, t):
        part = pl.ds(n * block, block)
        return remote(cg_half.at[part], cg_row.at[t - 1, part], h_s.at[n, t - 1], h_r.at[n, t - 1], row=(r + 2 * t) % nrow)

    for n in range(2):
        for t in range(1, nrow // 2):
            h_copy(n, t).start()

    fg_ref[...] = fg_scale * outer[0:rows, :]

    @pl.when(r == 0)
    def _():
        acc = outer[0:np_all, :] + inner[...]
        for e in range(1, nrow):
            remote(inner, inner_rec.at[e - 1], i_s.at[0], i_r.at[e - 1], row=e).wait_recv()
            acc = acc + inner_rec[e - 1]
        fg_ref[0:np_all, :] = fg_scale * acc

    fg_out = pltpu.make_async_copy(fg_ref, fg_hbm, out_s.at[1])
    fg_out.start()

    for c in range(len(spans)):
        for m in range(ngrid):
            keeps, far, near = p_copy(c, m)

            @pl.when(keeps != r)
            def _():
                far.wait_send()

            @pl.when(keeps == r)
            def _():
                near.wait()
    for src in range(nrow):
        @pl.when(r != src)
        def _():
            for t in range(per_row):
                for c, span in enumerate(spans):
                    here = prec.at[t, src, :, span]
                    remote(here, here, p_s.at[0, 0], p_r.at[c, t, src], row=src).wait_recv()

        for t in range(per_row):
            for i in range(npp):
                res_ref[pl.ds(src * rows * held + t * npp + i, rows, stride=held), :] = prec[t, src, i, 0:rows, :]

    res_out = pltpu.make_async_copy(res_ref, res_hbm, out_s.at[0])
    res_out.start()

    def f_copy(n):
        dst = cg_hbm.at[pl.ds(pl.multiple_of(odd * half + n * block, block), block)]
        return remote(cg_fin.at[n], dst, f_s.at[n], f_r.at[n], row=mate), pltpu.make_async_copy(cg_fin.at[n], dst, out_s.at[2 + n])

    for n in range(2):
        part = pl.ds(n * block, block)
        acc = cg_half[part, :]
        for t in range(1, nrow // 2):
            h_copy(n, t).wait_recv()
            acc = acc + cg_row[t - 1, part, :]
        cg_fin[n] = cg_scale * acc
        for copy in f_copy(n):
            copy.start()
    for n in range(2):
        here = cg_hbm.at[pl.ds(pl.multiple_of((1 - odd) * half + n * block, block), block)]
        remote(cg_fin.at[n], here, f_s.at[n], f_r.at[n], row=mate).wait_recv()

    @pl.when(r == 0)
    def _():
        for e in range(1, nrow):
            x8_copy(e).wait_send()

    @pl.when(r == owner)
    def _():
        for e in range(1, nrow):
            c_copy(e).wait_send()

    @pl.when(r != 0)
    def _():
        i_copy().wait_send()

    for c in range(len(spans)):
        for s in range(bits):
            for m in range(0, ngrid, 2 << s):
                rs_copy(c, s, m | 1 << s).wait_send()
                ag_copy(c, s, m).wait_send()
    for n in range(2):
        for t in range(1, nrow // 2):
            h_copy(n, t).wait_send()
        far, near = f_copy(n)
        far.wait_send()
        near.wait()
    k_copy.wait_send()
    res_out.wait()
    fg_out.wait()


def hand_out(res_in, cg_in, fg_in, res_out, cg_out, fg_out, res, cg, fg, sems):
    ways = []
    for src, mid, dst, axis, parts in ((res_in, res, res_out, 0, 6), (fg_in, fg, fg_out, 1, 3), (cg_in, cg, cg_out, 0, 3)):
        size = src.shape[axis] // parts
        for n in range(parts):
            part = (slice(None),) * axis + (pl.ds(n * size, size),)
            ways.append((src.at[part], mid.at[part], dst.at[part]))
    into = [pltpu.make_async_copy(src, mid, sems.at[0, n]) for n, (src, mid, _) in enumerate(ways)]
    out = [pltpu.make_async_copy(mid, dst, sems.at[1, n]) for n, (_, mid, dst) in enumerate(ways)]
    for copy in into:
        copy.start()
    for first, second in zip(into, out):
        first.wait()
        second.start()
    for copy in out:
        copy.wait()


def per_device(nrow, ngrid, cholesky, factor, core):
    held = cholesky.shape[0]
    rows, pts = factor.shape
    vec = core.shape[1]
    np_all = held * nrow
    npp = np_all // ngrid
    per_row = held // npp
    bits = ngrid.bit_length() - 1
    rpad = -(-rows // 16) * 16
    tiles = rpad // 16
    third = max(1, tiles // 6)
    less = (tiles - third) * 7 // 16
    sizes = [(tiles - third - less) * 16, less * 16, third * 16]
    chunks = [(0, sizes[0]), (sizes[0] + sizes[2], sizes[1]), (sizes[0], sizes[2])]
    plain = list(range(bits))
    orders = [plain, plain, plain[1:] + plain[:1]]
    cg_scale = -1.0 / math.sqrt(np_all * rows * nrow)
    fg_scale = -math.sqrt(pts * ngrid / (rows * nrow * vec))
    cfg = (nrow, bits, npp, held, rows, rpad, vec, chunks, orders, cg_scale, fg_scale)

    slab = jnp.swapaxes(cholesky.reshape(held, nrow * rows, vec), 0, 1).reshape(nrow * rows * held, vec)

    piece = (npp, rpad, vec)
    nc = len(chunks)
    dma = pltpu.SemaphoreType.DMA
    hbm = pl.BlockSpec(memory_space=pltpu.HBM)
    f32 = lambda *shape: pltpu.VMEM(shape, F32)
    b16 = lambda *shape: pltpu.VMEM(shape, BF16)
    pairs = max(nrow // 2 - 1, 1)
    scratch = [
        f32(rows, pts), f32(rpad, pts), f32(pts, vec), f32(nrow * rows * held, vec), b16(rpad, pts), b16(rpad, pts),
        f32(np_all, pts), f32(np_all, pts, vec),
        b16(ngrid, pts, npp * vec), b16(ngrid, pts, npp * vec),
        f32(vec, pts), b16(ngrid, npp * vec, pts), b16(ngrid, npp * vec, pts),
        f32(ngrid, *piece), f32(ngrid - 1, *piece), f32(nrow, *piece), f32(*piece),
        f32(ngrid, *piece), f32(per_row, nrow, *piece),
        f32(rpad, pts), f32(vec, pts), f32(pts, vec),
        f32(nrow * rows * held, vec), f32(rows, pts),
        f32(pts // 2, vec), f32(pts // 2, vec), f32(pairs, pts // 2, vec), f32(2, pts // 4, vec),
        f32(np_all, pts), f32(nrow - 1, np_all, pts),
        dma((4,)), dma((4,)), dma((nrow - 1,)), dma((1,)), dma((nrow - 1,)), dma((1,)),
        dma((nc, ngrid - 1)), dma((nc, ngrid - 1)), dma((nc, ngrid)), dma((nc, ngrid)),
        dma((nc, ngrid)), dma((nc, per_row, nrow)), dma((1,)), dma((nrow - 1,)),
        dma((1,)), dma((1,)), dma((2, pairs)), dma((2, pairs)), dma((2,)), dma((2,)),
    ]
    macs = 3 * rows * pts * np_all * vec
    results = (
        jax.ShapeDtypeStruct((nrow * rows * held, vec), F32),
        jax.ShapeDtypeStruct((pts, vec), F32),
        jax.ShapeDtypeStruct((rows, pts), F32),
    )
    made = pl.pallas_call(
        functools.partial(kernel, cfg),
        out_shape=results,
        in_specs=[hbm] * 3,
        out_specs=(hbm, hbm, hbm),
        scratch_shapes=scratch,
        cost_estimate=pl.CostEstimate(flops=6 * macs, bytes_accessed=8 * rows * pts, transcendentals=0),
        compiler_params=pltpu.CompilerParams(collective_id=0, has_side_effects=True, vmem_limit_bytes=62 * 2**20),
        name="hypercontraction",
    )(factor, core, slab)
    res, cg, fg = pl.pallas_call(
        hand_out,
        out_shape=results,
        in_specs=[pl.BlockSpec(memory_space=pl.ANY)] * 3,
        out_specs=(hbm, hbm, hbm),
        scratch_shapes=[f32(nrow * rows * held, vec), f32(pts, vec), f32(rows, pts), dma((2, 12))],
        name="hand_out",
    )(*made)
    res = jnp.swapaxes(res.reshape(nrow * rows, held, vec), 0, 1).reshape(held, nrow * rows * vec)
    return res, cg, fg


def solution(mesh):
    placed = (P("row", None), P("row", "grid"), P("grid", None))
    return jax.shard_map(
        functools.partial(per_device, mesh.shape["row"], mesh.shape["grid"]),
        mesh=mesh,
        in_specs=placed,
        out_specs=(P("row", None), P("grid", None), P("row", "grid")),
        check_vma=False,
    )
```
